32 devices in a mesh: member: 2 (over x), gx: 16 (over z, y, core).
Axes of the slice: x: 2, y: 2, z: 4, core: 2. Of those that a mesh axis runs over, the one named last changes fastest.
Arguments:
- analysis: bfloat16 [3, 4, 1536, 512], P(None, None, 'gx'), may hold values from -4 to 4
- zonal_waves: int32 [8, 16], P('member'), parts along dimension 0, may hold values from 0 to 511
- meridional_waves: int32 [8, 16], P('member'), parts along dimension 0, may hold values from 0 to 1535
- amplitude_codes: int32 [8, 16], P('member'), parts along dimension 0, may hold values from 1 to 8
Outputs:
- forecast: bfloat16 [6, 4, 512, 1536], P('member', None, 'gx'), parts along dimension 0
The draws below stay inside these ranges and needn't reach their ends.
There are 2 independent parts, one for each index of `member`. The reference program is written for one: setup_inputs(seed, part) draws one part's arguments, and reference() takes and returns one part's arrays. A program takes and returns all parts, laid end to end along the dimension named above; an argument that names none is the same for every part. Nothing has to cross between parts.
All inputs are finite; a program needn't handle non-finite values.
Results may differ from the reference program's by a relative error of at most 0.006.
Values may be sent and summed in bfloat16 or wider, within the bound.
A program may use at most 64 MiB of HBM per device.

```python
import math
import jax
import jax.numpy as jnp
from jax import lax

NY = 1536
LEV = 4
MODES = 16
STEPS = 4
NX = 512


def with_ends(entries, key, low, top_value):
    place = [jax.random.randint(jax.random.fold_in(key, axis), (), 0, length) for axis, length in enumerate(entries.shape)]
    main_axis = entries.shape.index(max(entries.shape))
    beside = place[:main_axis] + [(place[main_axis] + 1) % entries.shape[main_axis]] + place[main_axis + 1:]
    return entries.at[tuple(place)].set(low).at[tuple(beside)].set(top_value)


def levels(stream_key, dims, pieces, smallest, high):
    def one(position, blocks):
        steps = jax.random.uniform(jax.random.fold_in(jax.random.fold_in(stream_key, 6), position), (blocks,), jnp.float32, smallest / len(pieces), high / len(pieces))
        return jnp.repeat(jnp.exp(steps), dims[position] // blocks).reshape((-1,) + (1,) * (len(dims) - position - 1))

    factor_of = one(*pieces[0])
    for cut in pieces[1:]:
        factor_of = factor_of * one(*cut)
    return factor_of


def normal_values(stream_key, dims, scale, most, split=(), kind=jnp.bfloat16):
    values = jax.random.normal(stream_key, dims, jnp.float32) * scale
    if len(split) > 0:
        values = levels(stream_key, dims, split, -0.22, 0.18) * values
    return jnp.clip(values, min=-most, max=most).astype(kind)


def setup_inputs(seed: int = 0, part: int = 0) -> dict:
    splits = jax.random.split(jax.random.key(seed), 5)
    part_splits = jax.random.split(jax.random.fold_in(splits[4], part), 5)
    analysis = normal_values(splits[0], (3, LEV, NY, NX), 0.5, 4.0, ((2, 16),))
    zonal_waves = with_ends(jax.random.randint(part_splits[1], (LEV, MODES), 0, NX), jax.random.fold_in(part_splits[1], 1), 0, NX - 1).astype(jnp.int32)
    meridional_waves = with_ends(jax.random.randint(part_splits[2], (LEV, MODES), 0, NY), jax.random.fold_in(part_splits[2], 1), 0, NY - 1).astype(jnp.int32)
    amplitude_codes = with_ends(jax.random.randint(part_splits[3], (LEV, MODES), 1, 9), jax.random.fold_in(part_splits[3], 1), 1, 8).astype(jnp.int32)
    return {"analysis": analysis, "zonal_waves": zonal_waves, "meridional_waves": meridional_waves, "amplitude_codes": amplitude_codes}


TIME_STEP = 0.15
FILTER = 0.03
GRAVITY = 0.5
AMP_UNIT = 0.04


def take_cells(values, axis_dim, offset, length):
    return lax.slice_in_dim(values, offset, offset + length, axis=axis_dim)


def centred(quantity, axis_dim, length):
    near_pair = take_cells(quantity, axis_dim, 3, length) - take_cells(quantity, axis_dim, 1, length)
    far_pair = take_cells(quantity, axis_dim, 4, length) - take_cells(quantity, axis_dim, 0, length)
    return (8.0 * near_pair - far_pair) * (1.0 / 12.0)


def fourth(quantity, axis_dim, length):
    outer = take_cells(quantity, axis_dim, 0, length) + take_cells(quantity, axis_dim, 4, length)
    inner = take_cells(quantity, axis_dim, 1, length) + take_cells(quantity, axis_dim, 3, length)
    return outer - 4.0 * inner + 6.0 * take_cells(quantity, axis_dim, 2, length)


def advance(padded, lon_dim, lat_dim, lat_rows, lat_total):
    fields = padded.astype(jnp.float32)
    thickness, eastward, northward = fields[0], fields[1], fields[2]
    lon_axis = lon_dim - 1
    lat_axis = lat_dim - 1
    lon_count = thickness.shape[lon_axis] - 4
    lat_count = thickness.shape[lat_axis] - 4
    latitude = (math.pi / 3.0) * (2.0 * (lat_rows.astype(jnp.float32) + 0.5) / lat_total - 1.0)
    layout_shape = [1, 1, 1]
    layout_shape[lat_axis] = lat_count
    inverse = (1.0 / jnp.cos(latitude)).reshape(layout_shape)
    coriolis = (2.0 * jnp.sin(latitude)).reshape(layout_shape)
    pressure = GRAVITY * (0.5 * jnp.sum(thickness, axis=0, keepdims=True) + 0.5 * lax.cumsum(thickness, axis=0, reverse=True))

    def strip_lon(quantity):
        return take_cells(quantity, lat_axis, 2, lat_count)

    def strip_lat(quantity):
        return take_cells(quantity, lon_axis, 2, lon_count)

    def slope_lon(quantity):
        return centred(strip_lon(quantity), lon_axis, lon_count) * inverse

    def slope_lat(quantity):
        return centred(strip_lat(quantity), lat_axis, lat_count)

    def smooth(quantity):
        return fourth(strip_lon(quantity), lon_axis, lon_count) + fourth(strip_lat(quantity), lat_axis, lat_count)

    column = 1.0 + thickness
    thick_mid = strip_lon(strip_lat(thickness))
    east_mid = strip_lon(strip_lat(eastward))
    north_mid = strip_lon(strip_lat(northward))
    thick_tend = -(slope_lon(column * eastward) + slope_lat(column * northward))
    east_tend = -(east_mid * slope_lon(eastward) + north_mid * slope_lat(eastward)) - slope_lon(pressure) + coriolis * north_mid
    north_tend = -(east_mid * slope_lon(northward) + north_mid * slope_lat(northward)) - slope_lat(pressure) - coriolis * east_mid
    thick_new = thick_mid + TIME_STEP * thick_tend - FILTER * smooth(thickness)
    east_new = east_mid + TIME_STEP * east_tend - FILTER * smooth(eastward)
    north_new = north_mid + TIME_STEP * north_tend - FILTER * smooth(northward)
    return jnp.stack([thick_new, east_new, north_new], axis=0).astype(jnp.bfloat16)


def perturbation(lon_cells, lat_cells, zonal_waves, meridional_waves, amplitude_codes, lon_total, lat_total, lat_first):
    lon_phase = ((lon_cells[None, :, None] * zonal_waves[:, None, :]) % lon_total).astype(jnp.float32) * (2.0 * math.pi / lon_total)
    lat_phase = ((lat_cells[None, :, None] * meridional_waves[:, None, :]) % lat_total).astype(jnp.float32) * (2.0 * math.pi / lat_total)
    weights = (AMP_UNIT * amplitude_codes.astype(jnp.float32))[:, None, :]
    left_table = jnp.concatenate([weights * jnp.cos(lon_phase), -weights * jnp.sin(lon_phase)], axis=2)
    right_table = jnp.concatenate([jnp.cos(lat_phase), jnp.sin(lat_phase)], axis=2)
    if lat_first:
        return jnp.einsum("lym,lxm->lyx", right_table, left_table, precision=lax.Precision.HIGHEST)
    return jnp.einsum("lxm,lym->lxy", left_table, right_table, precision=lax.Precision.HIGHEST)


def reference(analysis, zonal_waves, meridional_waves, amplitude_codes):
    columns = jnp.transpose(analysis, (0, 1, 3, 2))
    lon_total = analysis.shape[3]
    lat_total = analysis.shape[2]
    lon_cells = jnp.arange(lon_total, dtype=jnp.int32)
    lat_cells = jnp.arange(lat_total, dtype=jnp.int32)
    added = perturbation(lon_cells, lat_cells, zonal_waves, meridional_waves, amplitude_codes, lon_total, lat_total, False)
    thickness = (columns[0].astype(jnp.float32) + added).astype(jnp.bfloat16)
    state = jnp.concatenate([thickness[None], columns[1:]], axis=0)
    for turn_index in range(STEPS):
        wrapped = jnp.concatenate([state[:, :, -2:], state, state[:, :, :2]], axis=2)
        padded = jnp.pad(wrapped, ((0, 0), (0, 0), (0, 0), (2, 2)))
        state = advance(padded, 2, 3, lat_cells, lat_total)
    return state
```

```python
import functools
import math

import jax
import jax.numpy as jnp
import numpy as np
from jax import lax
from jax.experimental import pallas as pl
from jax.experimental.pallas import tpu as pltpu
from jax.sharding import PartitionSpec as P

STEPS = 4
HALO = 2 * STEPS
TIME_STEP = 0.15
FILTER = 0.03
AMP_UNIT = 0.04
LANES = 128
MESH = pl.DeviceIdType.MESH


def ceil_to(value, unit):
    return -(-value // unit) * unit


def gather_kernel(n, members, x_ref, out_ref, send_ref, send_sem, recv_sem, fsend_sem, frecv_sem):
    comps, levels, own, nx = x_ref.shape
    width = nx // n
    total = out_ref.shape[1]
    half = ceil_to(own // 2, 16)
    me = lax.axis_index("gx")
    member = lax.axis_index("member")
    parity = lax.rem(member, 2)
    partner = member + 1 - 2 * parity

    barrier = pltpu.get_barrier_semaphore()
    for off in range(1, n):
        pl.semaphore_signal(
            barrier, inc=1, device_id=(member, lax.rem(me + off, n)), device_id_type=MESH
        )
    pl.semaphore_signal(barrier, inc=1, device_id=(partner, me), device_id_type=MESH)

    def columns(c, l, first, count):
        first = first % nx
        return x_ref[c, l, :, first : first + count]

    for t in range(n):
        for c in range(comps):
            main = [columns(c, l, t * width, width) for l in range(levels)]
            send_ref[t, c * own : (c + 1) * own, :] = jnp.concatenate(main, axis=1)
            edges = []
            for l in range(levels):
                edges.append(columns(c, l, t * width - HALO, HALO))
                edges.append(columns(c, l, (t + 1) * width, HALO))
            edge = jnp.concatenate(edges, axis=1)
            packed = jnp.concatenate([edge[:half], edge[own - half :]], axis=1)
            start = comps * own + c * half
            send_ref[t, start : start + half, :] = packed
    out_ref[me] = send_ref[me]
    pl.semaphore_wait(barrier, n)

    cut = ceil_to(total // 2, 16)
    parts = (pl.ds(0, cut), pl.ds(cut, total - cut))

    def exchange(mine, other):
        def spread(off):
            target = lax.rem(me + off, n)
            return pltpu.make_async_remote_copy(
                src_ref=send_ref.at[target, mine],
                dst_ref=out_ref.at[me, mine],
                send_sem=send_sem.at[off],
                recv_sem=recv_sem.at[off],
                device_id=(member, target),
                device_id_type=MESH,
            )

        def arrival(off):
            source = lax.rem(me + n - off, n)
            return pltpu.make_async_remote_copy(
                src_ref=send_ref.at[source, mine],
                dst_ref=out_ref.at[source, mine],
                send_sem=send_sem.at[off],
                recv_sem=recv_sem.at[off],
                device_id=(member, source),
                device_id_type=MESH,
            )

        def forward(off, rows):
            source = lax.rem(me + n - off, n)
            return pltpu.make_async_remote_copy(
                src_ref=out_ref.at[source, rows],
                dst_ref=out_ref.at[source, rows],
                send_sem=fsend_sem.at[off],
                recv_sem=frecv_sem.at[off],
                device_id=(partner, me),
                device_id_type=MESH,
            )

        for off in range(1, n):
            spread(off).start()
        for off in range(1, n):
            arrival(off).wait_recv()
            forward(off, mine).start()
        for off in range(1, n):
            forward(off, other).wait_recv()
        for off in range(1, n):
            spread(off).wait_send()
            forward(off, mine).wait_send()

    @pl.when(parity == 0)
    def _():
        exchange(parts[0], parts[1])

    @pl.when(parity == 1)
    def _():
        exchange(parts[1], parts[0])


def gather(analysis, n, members):
    comps, levels, own, nx = analysis.shape
    half = ceil_to(own // 2, 16)
    total = comps * (own + half)
    return pl.pallas_call(
        functools.partial(gather_kernel, n, members),
        out_shape=jax.ShapeDtypeStruct((n, total, LANES), jnp.bfloat16),
        in_specs=[pl.BlockSpec(memory_space=pltpu.VMEM)],
        out_specs=pl.BlockSpec(memory_space=pltpu.VMEM),
        scratch_shapes=[pltpu.VMEM((n, total, LANES), jnp.bfloat16)]
        + [pltpu.SemaphoreType.DMA((n,)) for _ in range(4)],
        compiler_params=pltpu.CompilerParams(
            collective_id=0, has_side_effects=True, vmem_limit_bytes=24 * 2**20
        ),
    )(analysis)


def placing(levels, width):
    wide = width + 2 * HALO
    table = np.zeros((levels * wide, 2 * LANES), np.float32)
    for l in range(levels):
        for x in range(wide):
            row = l * wide + x
            if HALO <= x < HALO + width:
                table[row, l * width + x - HALO] = 1.0
            else:
                e = x if x < HALO else x - width
                lane = l * 2 * HALO + e
                table[row, LANES + lane] = 1.0
                table[row, LANES + LANES // 2 + lane] = 1.0
    return table


def stencils(levels, wide):
    out = wide - 4
    one = {
        "mid": (0, 0, 1, 0, 0),
        "slope": (1, -8, 0, 8, -1),
        "smooth": (1, -4, 6, -4, 1),
    }
    mats = {}
    for name, taps in one.items():
        m = np.zeros((out, wide), np.float32)
        for x in range(out):
            m[x, x : x + 5] = taps
        mats[name] = m
    eye = np.eye(levels, dtype=np.float32)
    k = np.arange(levels)
    mix = 0.25 + 0.25 * (k[None, :] >= k[:, None]).astype(np.float32)
    mid, slope, smooth = (np.kron(eye, mats[s]) for s in ("mid", "slope", "smooth"))
    wind = np.concatenate([mid, slope, smooth])
    thick = np.concatenate([mid, np.kron(mix, mats["slope"]), smooth, np.kron(mix, mats["mid"])])
    flux = np.concatenate([slope, slope], axis=1)
    return wind, thick, flux


def steps_kernel(dims, r_ref, place_ref, left_ref, right_ref, geo_ref, *refs):
    n, comps, levels, own, half, width = dims
    mats = refs[: 3 * STEPS]
    out_ref = refs[3 * STEPS]
    state_ref, hu_ref, wu_ref, wv_ref, wh_ref, wf_ref = refs[3 * STEPS + 1 :]
    ny = n * own
    wide = width + 2 * HALO
    rows = levels * wide
    pad = wu_ref.shape[1]

    row_index = lax.broadcasted_iota(jnp.int32, (n, 2 * half, LANES), 1)
    lane_index = lax.broadcasted_iota(jnp.int32, (n, 2 * half, LANES), 2)
    keep = (row_index < half) == (lane_index < LANES // 2)
    added = jnp.dot(
        left_ref[...],
        right_ref[...],
        preferred_element_type=jnp.float32,
        precision=lax.Precision.HIGHEST,
    )
    for c in range(comps):
        main = r_ref[:, c * own : (c + 1) * own, :]
        start = comps * own + c * half
        edge = r_ref[:, start : start + half, :]
        both = jnp.concatenate([edge, edge], axis=1)
        both = jnp.where(keep, both, jnp.zeros_like(both))
        if 2 * half > own:
            both = jnp.concatenate(
                [both[:, : own - half], both[:, half:]], axis=1
            )
        block = jnp.concatenate([main, both], axis=2).reshape(ny, 2 * LANES)
        field = lax.dot_general(
            place_ref[...], block, (((1,), (1,)), ((), ())), preferred_element_type=jnp.float32
        )
        if c == 0:
            field = field + added
        state_ref[c, :rows, :] = field.astype(jnp.bfloat16)

    for ref in (wu_ref, wv_ref, wh_ref):
        ref[:, ny:] = jnp.zeros((ref.shape[0], pad - ny), jnp.float32)

    for step in range(STEPS):
        rows_in = levels * (wide - 4 * step)
        rows_out = levels * (wide - 4 * step - 4)
        wind, thick, flux = mats[3 * step : 3 * step + 3]
        product = state_ref[0, :rows_in, :].astype(jnp.float32) * state_ref[
            1, :rows_in, :
        ].astype(jnp.float32)
        high = product.astype(jnp.bfloat16)
        hu_ref[:rows_in, :] = high
        hu_ref[rows_in : 2 * rows_in, :] = (product - high.astype(jnp.float32)).astype(jnp.bfloat16)

        def times(m_ref, x, into):
            into[: m_ref.shape[0], :ny] = jnp.dot(
                m_ref[...], x, preferred_element_type=jnp.float32
            )

        times(wind, state_ref[1, :rows_in, :], wu_ref)
        times(wind, state_ref[2, :rows_in, :], wv_ref)
        times(thick, state_ref[0, :rows_in, :], wh_ref)
        times(flux, hu_ref[: 2 * rows_in, :], wf_ref)

        def group(g, carry, rows_out=rows_out, last=step == STEPS - 1):
            size = 16

            def part(ref, which, lanes=ny):
                first = pl.multiple_of(which * rows_out + g * size, size)
                return ref[pl.ds(first, size), :lanes]

            def around(x):
                return [pltpu.roll(x, s % pad, 1) for s in (2, 1, -1, -2)]

            def slope(near):
                return (8.0 * (near[2] - near[1]) - (near[3] - near[0]))[:, :ny]

            def fourth(x, near):
                return ((near[0] + near[3]) - 4.0 * (near[1] + near[2]) + 6.0 * x)[:, :ny]

            inv = geo_ref[0:1, :]
            cor = geo_ref[1:2, :]
            h, u, v, p = (
                part(wh_ref, 0, pad),
                part(wu_ref, 0, pad),
                part(wv_ref, 0, pad),
                part(wh_ref, 3, pad),
            )
            ha, ua, va = around(h), around(u), around(v)
            flux_y = slope([a + a * b for a, b in zip(va, ha)])
            press_y = slope(around(p))
            h_s, u_s, v_s = fourth(h, ha), fourth(u, ua), fourth(v, va)
            u_y, v_y = slope(ua), slope(va)
            h, u, v = h[:, :ny], u[:, :ny], v[:, :ny]
            u_x, v_x = part(wu_ref, 1), part(wv_ref, 1)
            ur = u * inv
            k = TIME_STEP / 12.0
            new_h = (
                h
                - k * (inv * (u_x + part(wf_ref, 0)) + flux_y)
                - FILTER * (h_s + part(wh_ref, 2))
            )
            new_u = (
                u
                - k * (ur * u_x + v * u_y + inv * part(wh_ref, 1))
                + cor * v
                - FILTER * (u_s + part(wu_ref, 2))
            )
            new_v = (
                v
                - k * (ur * v_x + v * v_y + press_y)
                - cor * u
                - FILTER * (v_s + part(wv_ref, 2))
            )
            here = pl.ds(pl.multiple_of(g * size, size), size)
            target = out_ref if last else state_ref
            for c, value in enumerate((new_h, new_u, new_v)):
                target[c, here, :] = value.astype(jnp.bfloat16)
            return carry

        lax.fori_loop(0, rows_out // 16, group, 0)


def tables(zonal, meridional, codes, place, nx, ny, width):
    levels = zonal.shape[0]
    lon = lax.rem(
        place * width - HALO + nx + jnp.arange(width + 2 * HALO, dtype=jnp.int32), nx
    )
    lat = jnp.arange(ny, dtype=jnp.int32)
    lon_phase = (lon[None, :, None] * zonal[:, None, :] % nx).astype(jnp.float32) * (
        2.0 * math.pi / nx
    )
    lat_phase = (meridional[:, :, None] * lat[None, None, :] % ny).astype(jnp.float32) * (
        2.0 * math.pi / ny
    )
    weights = (AMP_UNIT * codes.astype(jnp.float32))[:, None, :]
    left = jnp.concatenate([weights * jnp.cos(lon_phase), -weights * jnp.sin(lon_phase)], axis=2)
    right = jnp.concatenate([jnp.cos(lat_phase), jnp.sin(lat_phase)], axis=1)
    eye = jnp.eye(levels, dtype=jnp.float32)
    left = left[:, :, None, :] * eye[:, None, :, None]
    return left.reshape(-1, levels * left.shape[-1]), right.reshape(-1, ny)


def solution(mesh):
    n = mesh.shape["gx"]
    members = mesh.shape["member"]

    def shards(analysis, zonal, meridional, codes):
        comps, levels, own, nx = analysis.shape
        ny = n * own
        width = nx // n
        wide = width + 2 * HALO
        half = ceil_to(own // 2, 16)
        place = lax.axis_index("gx")
        left, right = tables(zonal, meridional, codes, place, nx, ny, width)
        lat = (math.pi / 3.0) * (2.0 * (np.arange(ny) + 0.5) / ny - 1.0)
        geo = np.stack([1.0 / np.cos(lat), TIME_STEP * 2.0 * np.sin(lat)]).astype(np.float32)
        mats = []
        for step in range(STEPS):
            mats += [jnp.asarray(m, jnp.bfloat16) for m in stencils(levels, wide - 4 * step)]
        received = gather(analysis, n, members)
        rows_in = levels * wide
        rows_out = rows_in - 4 * levels
        pad = ny + LANES
        vmem = pl.BlockSpec(memory_space=pltpu.VMEM)
        out = pl.pallas_call(
            functools.partial(steps_kernel, (n, comps, levels, own, half, width)),
            out_shape=jax.ShapeDtypeStruct((comps, levels * width, ny), jnp.bfloat16),
            in_specs=[vmem] * (5 + 3 * STEPS),
            out_specs=vmem,
            scratch_shapes=[
                pltpu.VMEM((comps, rows_in, ny), jnp.bfloat16),
                pltpu.VMEM((2 * rows_in, ny), jnp.bfloat16),
                pltpu.VMEM((3 * rows_out, pad), jnp.float32),
                pltpu.VMEM((3 * rows_out, pad), jnp.float32),
                pltpu.VMEM((4 * rows_out, pad), jnp.float32),
                pltpu.VMEM((rows_out, ny), jnp.float32),
            ],
            compiler_params=pltpu.CompilerParams(vmem_limit_bytes=48 * 2**20),
        )(
            received,
            jnp.asarray(placing(levels, width), jnp.bfloat16),
            left,
            right,
            jnp.asarray(geo),
            *mats,
        )
        return out.reshape(comps, levels, width, ny)

    placed = (P(None, None, "gx", None), P("member", None), P("member", None), P("member", None))
    return jax.shard_map(
        shards, mesh=mesh, in_specs=placed, out_specs=P("member", None, "gx", None), check_vma=False
    )
```

```python
import functools
import math

import jax
import jax.numpy as jnp
import numpy as np
from jax import lax
from jax.experimental import pallas as pl
from jax.experimental.pallas import tpu as pltpu
from jax.sharding import PartitionSpec as P

STEPS = 4
HALO = 2 * STEPS
TIME_STEP = 0.15
FILTER = 0.03
AMP_UNIT = 0.04
LANES = 128
MESH = pl.DeviceIdType.MESH


def ceil_to(value, unit):
    return -(-value // unit) * unit


def turns(product, count):
    rest = product - jnp.floor(product * (1.0 / count)) * count
    return rest * (2.0 * math.pi / count)


def waves(me, n, own, nx, width, levels, lon_ref, lat_ref):
    ny = n * own
    wide = width + 2 * HALO
    shape = (levels * wide, lon_ref.shape[1])
    row = lax.broadcasted_iota(jnp.int32, shape, 0)
    lane = lax.broadcasted_iota(jnp.int32, shape, 1)
    level = jnp.zeros(shape, jnp.int32)
    for l in range(1, levels):
        level = level + jnp.where(row >= l * wide, 1, 0)
    lon = row - level * wide + (me * width - HALO)
    lon = jnp.where(lon < 0, lon + nx, jnp.where(lon >= nx, lon - nx, lon))
    phase = turns(lon.astype(jnp.float32) * lon_ref[0:1, :], float(nx))
    count = shape[1] // 2
    modes = count // levels
    sine = lane >= count
    within = lane - jnp.where(sine, count, 0)
    own_level = (within >= level * modes) & (within < level * modes + modes)
    left = jnp.where(sine, -jnp.sin(phase), jnp.cos(phase)) * lon_ref[1:2, :]
    left = jnp.where(own_level, left, 0.0)
    lat = lax.broadcasted_iota(jnp.int32, (count, ny), 1).astype(jnp.float32)
    phase = turns(lat * lat_ref[...], float(ny))
    right = jnp.concatenate([jnp.cos(phase), jnp.sin(phase)], axis=0)
    return jnp.dot(
        left, right, preferred_element_type=jnp.float32, precision=lax.Precision.HIGHEST
    )


def gather_kernel(n, x_ref, lon_ref, lat_ref, out_ref, added_ref, send_ref, send_sem, recv_sem, fsend_sem, frecv_sem):
    comps, levels, own, nx = x_ref.shape
    width = nx // n
    total = out_ref.shape[1]
    half = ceil_to(own // 2, 16)
    me = lax.axis_index("gx")
    member = lax.axis_index("member")
    parity = lax.rem(member, 2)
    partner = member + 1 - 2 * parity

    barrier = pltpu.get_barrier_semaphore()
    for off in range(1, n):
        pl.semaphore_signal(
            barrier, inc=1, device_id=(member, lax.rem(me + off, n)), device_id_type=MESH
        )
    pl.semaphore_signal(barrier, inc=1, device_id=(partner, me), device_id_type=MESH)

    cut = ceil_to(total // 2, 16)
    parts = (pl.ds(0, cut), pl.ds(cut, total - cut))
    group = LANES // width
    tiles = nx // LANES
    mine_tile = lax.div(me, group)

    def flipped(value, bits):
        result = value
        b = 1
        while b <= bits:
            if bits & b:
                result = result + b * (1 - 2 * lax.rem(lax.div(value, b), 2))
            b *= 2
        return result

    def tile_columns(c, tile):
        first = pl.multiple_of(tile * LANES, LANES)
        return [x_ref[c, l, :, pl.ds(first, LANES)] for l in range(levels)]

    def pack(tile):
        before = lax.rem(tile + tiles - 1, tiles)
        after = lax.rem(tile + 1, tiles)
        for c in range(comps):
            here = tile_columns(c, tile)
            low = [x[:, LANES - HALO :] for x in tile_columns(c, before)]
            high = [x[:, :HALO] for x in tile_columns(c, after)]
            for d in range(group):
                t = tile * group + d
                first = d * width
                last = first + width
                main = [x[:, first:last] for x in here]
                send_ref[t, c * own : (c + 1) * own, :] = jnp.concatenate(main, axis=1)
                edges = []
                for l in range(levels):
                    edges.append(here[l][:, first - HALO : first] if d else low[l])
                    edges.append(here[l][:, last : last + HALO] if last < LANES else high[l])
                edge = jnp.concatenate(edges, axis=1)
                packed = jnp.concatenate([edge[:half], edge[own - half :]], axis=1)
                start = comps * own + c * half
                send_ref[t, start : start + half, :] = packed

    def spread(flip, mine):
        target = flipped(me, flip)
        return pltpu.make_async_remote_copy(
            src_ref=send_ref.at[target, mine],
            dst_ref=out_ref.at[me, mine],
            send_sem=send_sem.at[flip],
            recv_sem=recv_sem.at[flip],
            device_id=(member, target),
            device_id_type=MESH,
        )

    def arrival(flip, mine):
        source = flipped(me, flip)
        return pltpu.make_async_remote_copy(
            src_ref=send_ref.at[source, mine],
            dst_ref=out_ref.at[source, mine],
            send_sem=send_sem.at[flip],
            recv_sem=recv_sem.at[flip],
            device_id=(member, source),
            device_id_type=MESH,
        )

    def forward(flip, rows):
        source = flipped(me, flip)
        return pltpu.make_async_remote_copy(
            src_ref=out_ref.at[source, rows],
            dst_ref=out_ref.at[source, rows],
            send_sem=fsend_sem.at[flip],
            recv_sem=frecv_sem.at[flip],
            device_id=(partner, me),
            device_id_type=MESH,
        )

    order = []
    for tile_flip in range(tiles - 1, -1, -1):
        pack(flipped(mine_tile, tile_flip))
        if tile_flip == tiles - 1:
            pl.semaphore_wait(barrier, n)
        flips = [tile_flip * group + d for d in range(group - 1, -1, -1)]
        flips = [f for f in flips if f]
        order += flips
        for p in range(2):

            @pl.when(parity == p)
            def _(p=p, flips=flips):
                for f in flips:
                    spread(f, parts[p]).start()

    out_ref[me] = send_ref[me]
    added_ref[...] = waves(me, n, own, nx, width, levels, lon_ref, lat_ref)

    def exchange(mine, other):
        for f in order:
            arrival(f, mine).wait_recv()
            forward(f, mine).start()
        for f in order:
            forward(f, other).wait_recv()
        for f in order:
            spread(f, mine).wait_send()
            forward(f, mine).wait_send()

    @pl.when(parity == 0)
    def _():
        exchange(parts[0], parts[1])

    @pl.when(parity == 1)
    def _():
        exchange(parts[1], parts[0])


def gather(analysis, zonal, meridional, codes, n):
    comps, levels, own, nx = analysis.shape
    half = ceil_to(own // 2, 16)
    total = comps * (own + half)
    width = nx // n
    zonal = zonal.astype(jnp.float32).reshape(1, -1)
    weights = AMP_UNIT * codes.astype(jnp.float32).reshape(1, -1)
    lon_waves = jnp.tile(jnp.concatenate([zonal, weights], axis=0), (1, 2))
    lat_waves = meridional.astype(jnp.float32).reshape(-1, 1)
    vmem = pl.BlockSpec(memory_space=pltpu.VMEM)
    return pl.pallas_call(
        functools.partial(gather_kernel, n),
        out_shape=(
            jax.ShapeDtypeStruct((n, total, LANES), jnp.bfloat16),
            jax.ShapeDtypeStruct((levels * (width + 2 * HALO), n * own), jnp.float32),
        ),
        in_specs=[vmem] * 3,
        out_specs=(vmem, vmem),
        scratch_shapes=[pltpu.VMEM((n, total, LANES), jnp.bfloat16)]
        + [pltpu.SemaphoreType.DMA((n,)) for _ in range(4)],
        compiler_params=pltpu.CompilerParams(
            collective_id=0, has_side_effects=True, vmem_limit_bytes=24 * 2**20
        ),
    )(analysis, lon_waves, lat_waves)


def placing(levels, width):
    wide = width + 2 * HALO
    table = np.zeros((levels * wide, 2 * LANES), np.float32)
    for l in range(levels):
        for x in range(wide):
            row = l * wide + x
            if HALO <= x < HALO + width:
                table[row, l * width + x - HALO] = 1.0
            else:
                e = x if x < HALO else x - width
                lane = l * 2 * HALO + e
                table[row, LANES + lane] = 1.0
                table[row, LANES + LANES // 2 + lane] = 1.0
    return table


def stencils(levels, wide):
    out = wide - 4
    one = {
        "mid": (0, 0, 1, 0, 0),
        "slope": (1, -8, 0, 8, -1),
        "smooth": (1, -4, 6, -4, 1),
    }
    mats = {}
    for name, taps in one.items():
        m = np.zeros((out, wide), np.float32)
        for x in range(out):
            m[x, x : x + 5] = taps
        mats[name] = m
    eye = np.eye(levels, dtype=np.float32)
    k = np.arange(levels)
    mix = 0.25 + 0.25 * (k[None, :] >= k[:, None]).astype(np.float32)
    mid, slope, smooth = (np.kron(eye, mats[s]) for s in ("mid", "slope", "smooth"))
    wind = np.concatenate([mid, slope, smooth])
    thick = np.concatenate([mid, np.kron(mix, mats["slope"]), smooth, np.kron(mix, mats["mid"])])
    return wind, thick, slope


def steps_kernel(dims, r_ref, place_ref, added_ref, geo_ref, *refs):
    n, comps, levels, own, half, width = dims
    mats = refs[: 3 * STEPS]
    out_ref = refs[3 * STEPS]
    state_ref, hu_ref, wu_ref, wv_ref, wh_ref, wf_ref = refs[3 * STEPS + 1 :]
    ny = n * own
    wide = width + 2 * HALO
    rows = levels * wide
    pad = wu_ref.shape[1]

    row_index = lax.broadcasted_iota(jnp.int32, (n, 2 * half, LANES), 1)
    lane_index = lax.broadcasted_iota(jnp.int32, (n, 2 * half, LANES), 2)
    keep = (row_index < half) == (lane_index < LANES // 2)
    for c in range(comps):
        main = r_ref[:, c * own : (c + 1) * own, :]
        start = comps * own + c * half
        edge = r_ref[:, start : start + half, :]
        both = jnp.concatenate([edge, edge], axis=1)
        both = jnp.where(keep, both, jnp.zeros_like(both))
        if 2 * half > own:
            both = jnp.concatenate(
                [both[:, : own - half], both[:, half:]], axis=1
            )
        block = jnp.concatenate([main, both], axis=2).reshape(ny, 2 * LANES)
        field = lax.dot_general(
            place_ref[...], block, (((1,), (1,)), ((), ())), preferred_element_type=jnp.float32
        )
        if c == 0:
            field = field + added_ref[...]
        state_ref[c, :rows, :] = field.astype(jnp.bfloat16)

    for ref in (wu_ref, wv_ref, wh_ref):
        ref[:, ny:] = jnp.zeros((ref.shape[0], pad - ny), jnp.bfloat16)

    for step in range(STEPS):
        rows_in = levels * (wide - 4 * step)
        rows_out = levels * (wide - 4 * step - 4)
        wind, thick, flux = mats[3 * step : 3 * step + 3]
        column = 1.0 + state_ref[0, :rows_in, :].astype(jnp.float32)
        hu_ref[:rows_in, :] = (column * state_ref[1, :rows_in, :].astype(jnp.float32)).astype(
            jnp.bfloat16
        )

        def times(m_ref, x, into):
            into[: m_ref.shape[0], :ny] = jnp.dot(
                m_ref[...], x, preferred_element_type=jnp.float32
            ).astype(jnp.bfloat16)

        times(wind, state_ref[1, :rows_in, :], wu_ref)
        times(wind, state_ref[2, :rows_in, :], wv_ref)
        times(thick, state_ref[0, :rows_in, :], wh_ref)
        times(flux, hu_ref[:rows_in, :], wf_ref)

        def group(g, carry, rows_out=rows_out, last=step == STEPS - 1):
            size = 16

            def part(ref, which, lanes=ny):
                first = pl.multiple_of(which * rows_out + g * size, size)
                return ref[pl.ds(first, size), :lanes]

            def around(x):
                return [pltpu.roll(x, s % pad, 1) for s in (2, 1, -1, -2)]

            def slope(near):
                return (8.0 * (near[2] - near[1]) - (near[3] - near[0]))[:, :ny]

            def fourth(x, near):
                return ((near[0] + near[3]) - 4.0 * (near[1] + near[2]) + 6.0 * x)[:, :ny]

            inv = jnp.broadcast_to(geo_ref[0:1, :], (size, ny)).astype(jnp.bfloat16)
            cor = geo_ref[1:2, :]
            h, u, v, p = (
                part(wh_ref, 0, pad),
                part(wu_ref, 0, pad),
                part(wv_ref, 0, pad),
                part(wh_ref, 3, pad),
            )
            ha, ua, va = around(h), around(u), around(v)
            flux_y = slope([a + a * b for a, b in zip(va, ha)])
            press_y = slope(around(p))
            h_s, u_s, v_s = fourth(h, ha), fourth(u, ua), fourth(v, va)
            u_y, v_y = slope(ua), slope(va)
            h, u, v = h[:, :ny], u[:, :ny], v[:, :ny]
            u_x, v_x = part(wu_ref, 1), part(wv_ref, 1)
            ur = u * inv
            k = TIME_STEP / 12.0
            wide_type = jnp.float32
            h_t = inv * part(wf_ref, 0) + flux_y
            u_t = ur * u_x + v * u_y + inv * part(wh_ref, 1)
            v_t = ur * v_x + v * v_y + press_y
            h_s = h_s + part(wh_ref, 2)
            u_s = u_s + part(wu_ref, 2)
            v_s = v_s + part(wv_ref, 2)
            h, u, v, h_t, u_t, v_t, h_s, u_s, v_s = (
                x.astype(wide_type) for x in (h, u, v, h_t, u_t, v_t, h_s, u_s, v_s)
            )
            new_h = h - k * h_t - FILTER * h_s
            new_u = u - k * u_t + cor * v - FILTER * u_s
            new_v = v - k * v_t - cor * u - FILTER * v_s
            here = pl.ds(pl.multiple_of(g * size, size), size)
            target = out_ref if last else state_ref
            for c, value in enumerate((new_h, new_u, new_v)):
                target[c, here, :] = value.astype(jnp.bfloat16)
            return carry

        lax.fori_loop(0, rows_out // 16, group, 0)


def solution(mesh):
    n = mesh.shape["gx"]

    def shards(analysis, zonal, meridional, codes):
        comps, levels, own, nx = analysis.shape
        ny = n * own
        width = nx // n
        wide = width + 2 * HALO
        half = ceil_to(own // 2, 16)
        lat = (math.pi / 3.0) * (2.0 * (np.arange(ny) + 0.5) / ny - 1.0)
        geo = np.stack([1.0 / np.cos(lat), TIME_STEP * 2.0 * np.sin(lat)]).astype(np.float32)
        mats = []
        for step in range(STEPS):
            mats += [jnp.asarray(m, jnp.bfloat16) for m in stencils(levels, wide - 4 * step)]
        received, added = gather(analysis, zonal, meridional, codes, n)
        rows_in = levels * wide
        rows_out = rows_in - 4 * levels
        pad = ny + LANES
        vmem = pl.BlockSpec(memory_space=pltpu.VMEM)
        out = pl.pallas_call(
            functools.partial(steps_kernel, (n, comps, levels, own, half, width)),
            out_shape=jax.ShapeDtypeStruct((comps, levels * width, ny), jnp.bfloat16),
            in_specs=[vmem] * (4 + 3 * STEPS),
            out_specs=vmem,
            scratch_shapes=[
                pltpu.VMEM((comps, rows_in, ny), jnp.bfloat16),
                pltpu.VMEM((rows_in, ny), jnp.bfloat16),
                pltpu.VMEM((3 * rows_out, pad), jnp.bfloat16),
                pltpu.VMEM((3 * rows_out, pad), jnp.bfloat16),
                pltpu.VMEM((4 * rows_out, pad), jnp.bfloat16),
                pltpu.VMEM((rows_out, ny), jnp.bfloat16),
            ],
            compiler_params=pltpu.CompilerParams(vmem_limit_bytes=48 * 2**20),
        )(
            received,
            jnp.asarray(placing(levels, width), jnp.bfloat16),
            added,
            jnp.asarray(geo),
            *mats,
        )
        return out.reshape(comps, levels, width, ny)

    placed = (P(None, None, "gx", None), P("member", None), P("member", None), P("member", None))
    return jax.shard_map(
        shards, mesh=mesh, in_specs=placed, out_specs=P("member", None, "gx", None), check_vma=False
    )
```

```python
import functools
import math

import jax
import jax.numpy as jnp
from jax import lax
from jax.experimental import pallas as pl
from jax.experimental.pallas import tpu as pltpu
from jax.sharding import PartitionSpec as P

STEPS = 4
HALO = 2 * STEPS
TIME_STEP = 0.15
FILTER = 0.03
AMP_UNIT = 0.04
LANES = 128
MESH = pl.DeviceIdType.MESH


def ceil_to(value, unit):
    return -(-value // unit) * unit


def turns(product, count):
    rest = product - jnp.floor(product * (1.0 / count)) * count
    return rest * (2.0 * math.pi / count)


def waves(me, n, own, nx, width, levels, zonal, meridional, codes):
    def in_row(x):
        x = x.astype(jnp.float32)
        return jnp.concatenate([x[l : l + 1, :] for l in range(levels)], axis=1)

    zonal, meridional, codes = in_row(zonal), in_row(meridional), in_row(codes)
    count = zonal.shape[1]
    square = (count, count)
    diagonal = lax.broadcasted_iota(jnp.int32, square, 0) == lax.broadcasted_iota(
        jnp.int32, square, 1
    )
    meridional = jnp.sum(
        jnp.where(diagonal, jnp.broadcast_to(meridional, square), 0.0), axis=1, keepdims=True
    )
    zonal = jnp.concatenate([zonal, zonal], axis=1)
    weights = AMP_UNIT * jnp.concatenate([codes, codes], axis=1)
    ny = n * own
    wide = width + 2 * HALO
    shape = (levels * wide, 2 * count)
    row = lax.broadcasted_iota(jnp.int32, shape, 0)
    lane = lax.broadcasted_iota(jnp.int32, shape, 1)
    level = jnp.zeros(shape, jnp.int32)
    for l in range(1, levels):
        level = level + jnp.where(row >= l * wide, 1, 0)
    lon = row - level * wide + (me * width - HALO)
    lon = jnp.where(lon < 0, lon + nx, jnp.where(lon >= nx, lon - nx, lon))
    phase = turns(lon.astype(jnp.float32) * zonal, float(nx))
    modes = count // levels
    sine = lane >= count
    within = lane - jnp.where(sine, count, 0)
    own_level = (within >= level * modes) & (within < level * modes + modes)
    left = jnp.where(sine, -jnp.sin(phase), jnp.cos(phase)) * weights
    left = jnp.where(own_level, left, 0.0)
    lat = lax.broadcasted_iota(jnp.int32, (count, ny), 1).astype(jnp.float32)
    phase = turns(lat * meridional, float(ny))
    right = jnp.concatenate([jnp.cos(phase), jnp.sin(phase)], axis=0)
    return jnp.dot(
        left, right, preferred_element_type=jnp.float32, precision=lax.Precision.HIGHEST
    )


def gather_kernel(
    n,
    x_ref,
    zonal_ref,
    meridional_ref,
    codes_ref,
    out_ref,
    added_ref,
    mats_ref,
    place_ref,
    geo_ref,
    send_ref,
    send_sem,
    recv_sem,
    fsend_sem,
    frecv_sem,
):
    comps, levels, own, nx = x_ref.shape
    width = nx // n
    total = out_ref.shape[1]
    half = ceil_to(own // 2, 16)
    me = lax.axis_index("gx")
    member = lax.axis_index("member")
    parity = lax.rem(member, 2)
    partner = member + 1 - 2 * parity

    barrier = pltpu.get_barrier_semaphore()
    for off in range(1, n):
        pl.semaphore_signal(
            barrier, inc=1, device_id=(member, lax.rem(me + off, n)), device_id_type=MESH
        )
    pl.semaphore_signal(barrier, inc=1, device_id=(partner, me), device_id_type=MESH)

    cut = ceil_to(total // 2, 16)
    parts = (pl.ds(0, cut), pl.ds(cut, total - cut))
    group = LANES // width
    tiles = nx // LANES
    mine_tile = lax.div(me, group)

    def flipped(value, bits):
        result = value
        b = 1
        while b <= bits:
            if bits & b:
                result = result + b * (1 - 2 * lax.rem(lax.div(value, b), 2))
            b *= 2
        return result

    def tile_columns(c, tile):
        first = pl.multiple_of(tile * LANES, LANES)
        return [x_ref[c, l, :, pl.ds(first, LANES)] for l in range(levels)]

    def pack(tile):
        before = lax.rem(tile + tiles - 1, tiles)
        after = lax.rem(tile + 1, tiles)
        for c in range(comps):
            here = tile_columns(c, tile)
            low = [x[:, LANES - HALO :] for x in tile_columns(c, before)]
            high = [x[:, :HALO] for x in tile_columns(c, after)]
            for d in range(group):
                t = tile * group + d
                first = d * width
                last = first + width
                main = [x[:, first:last] for x in here]
                send_ref[t, c * own : (c + 1) * own, :] = jnp.concatenate(main, axis=1)
                edges = []
                for l in range(levels):
                    edges.append(here[l][:, first - HALO : first] if d else low[l])
                    edges.append(here[l][:, last : last + HALO] if last < LANES else high[l])
                edge = jnp.concatenate(edges, axis=1)
                packed = jnp.concatenate([edge[:half], edge[own - half :]], axis=1)
                start = comps * own + c * half
                send_ref[t, start : start + half, :] = packed

    def spread(flip, mine):
        target = flipped(me, flip)
        return pltpu.make_async_remote_copy(
            src_ref=send_ref.at[target, mine],
            dst_ref=out_ref.at[me, mine],
            send_sem=send_sem.at[flip],
            recv_sem=recv_sem.at[flip],
            device_id=(member, target),
            device_id_type=MESH,
        )

    def arrival(flip, mine):
        source = flipped(me, flip)
        return pltpu.make_async_remote_copy(
            src_ref=send_ref.at[source, mine],
            dst_ref=out_ref.at[source, mine],
            send_sem=send_sem.at[flip],
            recv_sem=recv_sem.at[flip],
            device_id=(member, source),
            device_id_type=MESH,
        )

    def forward(flip, rows):
        source = flipped(me, flip)
        return pltpu.make_async_remote_copy(
            src_ref=out_ref.at[source, rows],
            dst_ref=out_ref.at[source, rows],
            send_sem=fsend_sem.at[flip],
            recv_sem=frecv_sem.at[flip],
            device_id=(partner, me),
            device_id_type=MESH,
        )

    order = []
    for tile_flip in range(tiles - 1, -1, -1):
        pack(flipped(mine_tile, tile_flip))
        if tile_flip == tiles - 1:
            pl.semaphore_wait(barrier, n)
        flips = [tile_flip * group + d for d in range(group - 1, -1, -1)]
        flips = [f for f in flips if f]
        order += flips
        for p in range(2):

            @pl.when(parity == p)
            def _(p=p, flips=flips):
                for f in flips:
                    spread(f, parts[p]).start()

    near = [f for f in order if f < n // 2][::-1]
    far = [f for f in order if f >= n // 2]

    def early(mine):
        for f in near[: group - 1]:
            arrival(f, mine).wait_recv()
            forward(f, mine).start()

    for p in range(2):
        pl.when(parity == p)(functools.partial(early, parts[p]))
    out_ref[me] = send_ref[me]
    place_ref[...] = placing(levels, width)
    geo_ref[...] = geometry(n * own)
    base = 0
    for step in range(STEPS):
        for block in stencils(levels, width + 2 * HALO - 4 * step):
            mats_ref[base : base + block.shape[0], : block.shape[1]] = block
            base += block.shape[0]
    added_ref[...] = waves(
        me, n, own, nx, width, levels, zonal_ref[...], meridional_ref[...], codes_ref[...]
    )

    def exchange(mine, other):
        pending = near[group - 1 :]
        for i, f in enumerate(far):
            if i < len(pending):
                arrival(pending[i], mine).wait_recv()
                forward(pending[i], mine).start()
            arrival(f, mine).wait_recv()
            forward(f, mine).start()
        for f in order:
            forward(f, other).wait_recv()
        for f in order:
            spread(f, mine).wait_send()
            forward(f, mine).wait_send()

    @pl.when(parity == 0)
    def _():
        exchange(parts[0], parts[1])

    @pl.when(parity == 1)
    def _():
        exchange(parts[1], parts[0])


def gather(analysis, zonal, meridional, codes, n):
    comps, levels, own, nx = analysis.shape
    half = ceil_to(own // 2, 16)
    total = comps * (own + half)
    width = nx // n
    rows = levels * (width + 2 * HALO)
    mat_rows = sum(5 * (rows - 4 * levels * (step + 1)) for step in range(STEPS))
    vmem = pl.BlockSpec(memory_space=pltpu.VMEM)
    return pl.pallas_call(
        functools.partial(gather_kernel, n),
        out_shape=(
            jax.ShapeDtypeStruct((n, total, LANES), jnp.bfloat16),
            jax.ShapeDtypeStruct((rows, n * own), jnp.float32),
            jax.ShapeDtypeStruct((mat_rows, rows), jnp.bfloat16),
            jax.ShapeDtypeStruct((rows, 2 * LANES), jnp.bfloat16),
            jax.ShapeDtypeStruct((2, n * own), jnp.float32),
        ),
        in_specs=[vmem] * 4,
        out_specs=(vmem,) * 5,
        scratch_shapes=[pltpu.VMEM((n, total, LANES), jnp.bfloat16)]
        + [pltpu.SemaphoreType.DMA((n,)) for _ in range(4)],
        compiler_params=pltpu.CompilerParams(
            collective_id=0, has_side_effects=True, vmem_limit_bytes=24 * 2**20
        ),
    )(analysis, zonal, meridional, codes)


def level_and_column(shape, axis, levels, wide):
    index = lax.broadcasted_iota(jnp.int32, shape, axis)
    level = jnp.zeros(shape, jnp.int32)
    for l in range(1, levels):
        level = level + jnp.where(index >= l * wide, 1, 0)
    return level, index - level * wide


def placing(levels, width):
    wide = width + 2 * HALO
    shape = (levels * wide, 2 * LANES)
    level, x = level_and_column(shape, 0, levels, wide)
    lane = lax.broadcasted_iota(jnp.int32, shape, 1)
    inside = (x >= HALO) & (x < HALO + width)
    main = level * width + x - HALO
    edge = LANES + level * 2 * HALO + jnp.where(x < HALO, x, x - width)
    hit = (lane == jnp.where(inside, main, edge)) | (
        jnp.logical_not(inside) & (lane == edge + LANES // 2)
    )
    return jnp.where(hit, 1.0, 0.0).astype(jnp.bfloat16)


def stencils(levels, wide):
    out = wide - 4
    shape = (levels * out, levels * wide)
    level, x = level_and_column(shape, 0, levels, out)
    from_level, from_x = level_and_column(shape, 1, levels, wide)
    step = from_x - x

    def taps(*values):
        result = jnp.zeros(shape, jnp.float32)
        for i, value in enumerate(values):
            if value:
                result = jnp.where(step == i, float(value), result)
        return result

    same = jnp.where(level == from_level, 1.0, 0.0)
    mix = jnp.where(from_level >= level, 0.5, 0.25)
    slope, mid, smooth = taps(1, -8, 0, 8, -1), taps(0, 0, 1), taps(1, -4, 6, -4, 1)
    blocks = (slope * same, mid * same, smooth * same, slope * mix, mid * mix)
    return [b.astype(jnp.bfloat16) for b in blocks]


def geometry(ny):
    lat = lax.broadcasted_iota(jnp.int32, (1, ny), 1).astype(jnp.float32)
    lat = (math.pi / 3.0) * (2.0 * (lat + 0.5) / ny - 1.0)
    return jnp.concatenate([1.0 / jnp.cos(lat), (2.0 * TIME_STEP) * jnp.sin(lat)], axis=0)


def steps_kernel(dims, r_ref, added_ref, mats_ref, place_ref, geo_ref, out_ref, *refs):
    n, comps, levels, own, half, width = dims
    state_ref, hu_ref, wu_ref, wv_ref, wh_ref, wf_ref = refs
    ny = n * own
    wide = width + 2 * HALO
    rows = levels * wide
    pad = wu_ref.shape[1]

    row_index = lax.broadcasted_iota(jnp.int32, (n, 2 * half, LANES), 1)
    lane_index = lax.broadcasted_iota(jnp.int32, (n, 2 * half, LANES), 2)
    keep = (row_index < half) == (lane_index < LANES // 2)
    for c in range(comps):
        main = r_ref[:, c * own : (c + 1) * own, :]
        start = comps * own + c * half
        edge = r_ref[:, start : start + half, :]
        both = jnp.concatenate([edge, edge], axis=1)
        both = jnp.where(keep, both, jnp.zeros_like(both))
        if 2 * half > own:
            both = jnp.concatenate(
                [both[:, : own - half], both[:, half:]], axis=1
            )
        block = jnp.concatenate([main, both], axis=2).reshape(ny, 2 * LANES)
        field = lax.dot_general(
            place_ref[...], block, (((1,), (1,)), ((), ())), preferred_element_type=jnp.float32
        )
        if c == 0:
            field = field + added_ref[...]
        state_ref[c, :rows, :] = field.astype(jnp.bfloat16)

    for ref in (wu_ref, wv_ref, wh_ref):
        ref[:, ny:] = jnp.zeros((ref.shape[0], pad - ny), jnp.bfloat16)

    base = 0
    for step in range(STEPS):
        rows_in = levels * (wide - 4 * step)
        rows_out = levels * (wide - 4 * step - 4)
        slope_at, mid_at, last_at = base, base + rows_out, base + 5 * rows_out
        wind = mats_ref[slope_at : slope_at + 3 * rows_out, :rows_in]
        thick = mats_ref[mid_at:last_at, :rows_in]
        flux = mats_ref[slope_at:mid_at, :rows_in]
        base = last_at
        column = 1.0 + state_ref[0, :rows_in, :].astype(jnp.float32)
        hu_ref[:rows_in, :] = (column * state_ref[1, :rows_in, :].astype(jnp.float32)).astype(
            jnp.bfloat16
        )

        def times(matrix, x, into):
            into[: matrix.shape[0], :ny] = jnp.dot(
                matrix, x, preferred_element_type=jnp.float32
            ).astype(jnp.bfloat16)

        times(wind, state_ref[1, :rows_in, :], wu_ref)
        times(wind, state_ref[2, :rows_in, :], wv_ref)
        times(thick, state_ref[0, :rows_in, :], wh_ref)
        times(flux, hu_ref[:rows_in, :], wf_ref)

        def group(g, carry, rows_out=rows_out, last=step == STEPS - 1):
            size = 16

            def part(ref, which, lanes=ny):
                first = pl.multiple_of(which * rows_out + g * size, size)
                return ref[pl.ds(first, size), :lanes]

            def around(x):
                return [pltpu.roll(x, s % pad, 1) for s in (2, 1, -1, -2)]

            def slope(near):
                return (8.0 * (near[2] - near[1]) - (near[3] - near[0]))[:, :ny]

            def fourth(x, near):
                return ((near[0] + near[3]) - 4.0 * (near[1] + near[2]) + 6.0 * x)[:, :ny]

            inv = jnp.broadcast_to(geo_ref[0:1, :], (size, ny)).astype(jnp.bfloat16)
            cor = geo_ref[1:2, :]
            h, u, v, p = (
                part(wh_ref, 0, pad),
                part(wu_ref, 1, pad),
                part(wv_ref, 1, pad),
                part(wh_ref, 3, pad),
            )
            ha, ua, va = around(h), around(u), around(v)
            flux_y = slope([a + a * b for a, b in zip(va, ha)])
            press_y = slope(around(p))
            h_s, u_s, v_s = fourth(h, ha), fourth(u, ua), fourth(v, va)
            u_y, v_y = slope(ua), slope(va)
            h, u, v = h[:, :ny], u[:, :ny], v[:, :ny]
            u_x, v_x = part(wu_ref, 0), part(wv_ref, 0)
            ur = u * inv
            k = TIME_STEP / 12.0
            wide_type = jnp.float32
            h_t = inv * part(wf_ref, 0) + flux_y
            u_t = ur * u_x + v * u_y + inv * part(wh_ref, 2)
            v_t = ur * v_x + v * v_y + press_y
            h_s = h_s + part(wh_ref, 1)
            u_s = u_s + part(wu_ref, 2)
            v_s = v_s + part(wv_ref, 2)
            h, u, v, h_t, u_t, v_t, h_s, u_s, v_s = (
                x.astype(wide_type) for x in (h, u, v, h_t, u_t, v_t, h_s, u_s, v_s)
            )
            new_h = h - k * h_t - FILTER * h_s
            new_u = u - k * u_t + cor * v - FILTER * u_s
            new_v = v - k * v_t - cor * u - FILTER * v_s
            here = pl.ds(pl.multiple_of(g * size, size), size)
            target = out_ref if last else state_ref
            for c, value in enumerate((new_h, new_u, new_v)):
                target[c, here, :] = value.astype(jnp.bfloat16)
            return carry

        lax.fori_loop(0, rows_out // 16, group, 0)


def solution(mesh):
    n = mesh.shape["gx"]

    def shards(analysis, zonal, meridional, codes):
        comps, levels, own, nx = analysis.shape
        ny = n * own
        width = nx // n
        wide = width + 2 * HALO
        half = ceil_to(own // 2, 16)
        gathered = gather(analysis, zonal, meridional, codes, n)
        rows_in = levels * wide
        rows_out = rows_in - 4 * levels
        pad = ny + LANES
        vmem = pl.BlockSpec(memory_space=pltpu.VMEM)
        out = pl.pallas_call(
            functools.partial(steps_kernel, (n, comps, levels, own, half, width)),
            out_shape=jax.ShapeDtypeStruct((comps, levels * width, ny), jnp.bfloat16),
            in_specs=[vmem] * 5,
            out_specs=vmem,
            scratch_shapes=[
                pltpu.VMEM((comps, rows_in, ny), jnp.bfloat16),
                pltpu.VMEM((rows_in, ny), jnp.bfloat16),
                pltpu.VMEM((3 * rows_out, pad), jnp.bfloat16),
                pltpu.VMEM((3 * rows_out, pad), jnp.bfloat16),
                pltpu.VMEM((4 * rows_out, pad), jnp.bfloat16),
                pltpu.VMEM((rows_out, ny), jnp.bfloat16),
            ],
            compiler_params=pltpu.CompilerParams(vmem_limit_bytes=48 * 2**20),
        )(*gathered)
        return out.reshape(comps, levels, width, ny)

    placed = (P(None, None, "gx", None), P("member", None), P("member", None), P("member", None))
    return jax.shard_map(
        shards, mesh=mesh, in_specs=placed, out_specs=P("member", None, "gx", None), check_vma=False
    )
```

```python
import functools
import math

import jax
import jax.numpy as jnp
from jax import lax
from jax.experimental import pallas as pl
from jax.experimental.pallas import tpu as pltpu
from jax.sharding import PartitionSpec as P

STEPS = 4
HALO = 2 * STEPS
WINDOW = 3
TIME_STEP = 0.15
FILTER = 0.03
AMP_UNIT = 0.04
LANES = 128
MESH = pl.DeviceIdType.MESH


def ceil_to(value, unit):
    return -(-value // unit) * unit


def turns(product, count):
    rest = product - jnp.floor(product * (1.0 / count)) * count
    return rest * (2.0 * math.pi / count)


def in_row(x, levels):
    x = x.astype(jnp.float32)
    return jnp.concatenate([x[l : l + 1, :] for l in range(levels)], axis=1)


def waves_left(me, nx, width, levels, zonal, codes):
    zonal, codes = in_row(zonal, levels), in_row(codes, levels)
    count = zonal.shape[1]
    zonal = jnp.concatenate([zonal, zonal], axis=1)
    weights = AMP_UNIT * jnp.concatenate([codes, codes], axis=1)
    wide = width + 2 * HALO
    shape = (levels * wide, 2 * count)
    level, x = level_and_column(shape, 0, levels, wide)
    lane = lax.broadcasted_iota(jnp.int32, shape, 1)
    lon = x + (me * width - HALO)
    lon = jnp.where(lon < 0, lon + nx, jnp.where(lon >= nx, lon - nx, lon))
    phase = turns(lon.astype(jnp.float32) * zonal, float(nx))
    modes = count // levels
    sine = lane >= count
    within = lane - jnp.where(sine, count, 0)
    own_level = (within >= level * modes) & (within < level * modes + modes)
    left = jnp.where(sine, -jnp.sin(phase), jnp.cos(phase)) * weights
    return jnp.where(own_level, left, 0.0)


def waves_right(ny, levels, meridional):
    meridional = in_row(meridional, levels)
    count = meridional.shape[1]
    square = (count, count)
    diagonal = lax.broadcasted_iota(jnp.int32, square, 0) == lax.broadcasted_iota(
        jnp.int32, square, 1
    )
    meridional = jnp.sum(
        jnp.where(diagonal, jnp.broadcast_to(meridional, square), 0.0), axis=1, keepdims=True
    )
    lat = lax.broadcasted_iota(jnp.int32, (count, ny), 1).astype(jnp.float32)
    phase = turns(lat * meridional, float(ny))
    return jnp.concatenate([jnp.cos(phase), jnp.sin(phase)], axis=0)


def gather_kernel(
    n,
    x_hbm,
    zonal_hbm,
    meridional_hbm,
    codes_hbm,
    out_ref,
    added_ref,
    mats_ref,
    place_ref,
    geo_ref,
    send_ref,
    send_sem,
    recv_sem,
    fsend_sem,
    frecv_sem,
    x_ref,
    zonal_ref,
    meridional_ref,
    codes_ref,
    left_ref,
    right_ref,
    in_sem,
):
    comps, levels, own, nx = x_ref.shape
    width = nx // n
    total = out_ref.shape[1]
    half = ceil_to(own // 2, 16)
    me = lax.axis_index("gx")
    member = lax.axis_index("member")
    parity = lax.rem(member, 2)
    partner = member + 1 - 2 * parity

    barrier = pltpu.get_barrier_semaphore()
    for off in range(1, n):
        pl.semaphore_signal(
            barrier, inc=1, device_id=(member, lax.rem(me + off, n)), device_id_type=MESH
        )
    pl.semaphore_signal(barrier, inc=1, device_id=(partner, me), device_id_type=MESH)

    size = total // 2
    mine = pl.ds(pl.multiple_of(parity * size, 16), size)
    other = pl.ds(pl.multiple_of((1 - parity) * size, 16), size)
    group = LANES // width
    tiles = nx // LANES
    mine_tile = lax.div(me, group)

    loads = [
        pltpu.make_async_copy(source, target, in_sem.at[i])
        for i, (source, target) in enumerate(
            (
                (x_hbm, x_ref),
                (zonal_hbm, zonal_ref),
                (meridional_hbm, meridional_ref),
                (codes_hbm, codes_ref),
            )
        )
    ]
    for load in loads:
        load.start()
    for load in loads:
        load.wait()
    used = comps * (own + half)
    if total > used:
        send_ref[:, used:, :] = jnp.zeros((n, total - used, LANES), jnp.bfloat16)

    def flipped(value, bits):
        result = value
        b = 1
        while b <= bits:
            if bits & b:
                result = result + b * (1 - 2 * lax.rem(lax.div(value, b), 2))
            b *= 2
        return result

    def tile_columns(c, tile):
        first = pl.multiple_of(tile * LANES, LANES)
        return [x_ref[c, l, :, pl.ds(first, LANES)] for l in range(levels)]

    def pack(tile):
        before = lax.rem(tile + tiles - 1, tiles)
        after = lax.rem(tile + 1, tiles)
        for c in range(comps):
            here = tile_columns(c, tile)
            low = [x[:, LANES - HALO :] for x in tile_columns(c, before)]
            high = [x[:, :HALO] for x in tile_columns(c, after)]
            for d in range(group):
                t = tile * group + d
                first = d * width
                last = first + width
                main = [x[:, first:last] for x in here]
                send_ref[t, c * own : (c + 1) * own, :] = jnp.concatenate(main, axis=1)
                edges = []
                for l in range(levels):
                    edges.append(here[l][:, first - HALO : first] if d else low[l])
                    edges.append(here[l][:, last : last + HALO] if last < LANES else high[l])
                edge = jnp.concatenate(edges, axis=1)
                packed = jnp.concatenate([edge[:half], edge[own - half :]], axis=1)
                start = comps * own + c * half
                send_ref[t, start : start + half, :] = packed

    def spread(flip):
        target = flipped(me, flip)
        return pltpu.make_async_remote_copy(
            src_ref=send_ref.at[target, mine],
            dst_ref=out_ref.at[me, mine],
            send_sem=send_sem.at[flip],
            recv_sem=recv_sem.at[flip],
            device_id=(member, target),
            device_id_type=MESH,
        )

    def arrival(flip):
        source = flipped(me, flip)
        return pltpu.make_async_remote_copy(
            src_ref=send_ref.at[source, mine],
            dst_ref=out_ref.at[source, mine],
            send_sem=send_sem.at[flip],
            recv_sem=recv_sem.at[flip],
            device_id=(member, source),
            device_id_type=MESH,
        )

    def forward(flip, rows):
        source = flipped(me, flip)
        return pltpu.make_async_remote_copy(
            src_ref=out_ref.at[source, rows],
            dst_ref=out_ref.at[source, rows],
            send_sem=fsend_sem.at[flip],
            recv_sem=frecv_sem.at[flip],
            device_id=(partner, me),
            device_id_type=MESH,
        )

    order = []
    for tile_flip in range(tiles - 1, -1, -1):
        pack(flipped(mine_tile, tile_flip))
        flips = [tile_flip * group + d for d in range(group - 1, -1, -1)]
        flips = [f for f in flips if f]
        order += flips
        if tile_flip == tiles - 1:
            pl.semaphore_wait(barrier, n)
            for f in flips[:WINDOW]:
                spread(f).start()
        if tile_flip < tiles // 2:
            for f in flips:
                spread(f).start()
    out_ref[me] = send_ref[me]

    near = [f for f in order if f < n // 2][::-1]
    far = [f for f in order if f >= n // 2]

    def pass_on(flip):
        arrival(flip).wait_recv()
        forward(flip, mine).start()

    starts = [0]
    for step in range(STEPS):
        rows = levels * (width + 2 * HALO - 4 * step - 4)
        starts.append(starts[-1] + 5 * rows)

    def matrices(step):
        base = starts[step]
        for block in stencils(levels, width + 2 * HALO - 4 * step):
            mats_ref[base : base + block.shape[0], : block.shape[1]] = block
            base += block.shape[0]

    def small():
        place_ref[...] = placing(levels, width)
        geo_ref[...] = geometry(n * own)

    def left():
        left_ref[...] = waves_left(me, nx, width, levels, zonal_ref[...], codes_ref[...])

    def right():
        right_ref[...] = waves_right(n * own, levels, meridional_ref[...])

    def added():
        added_ref[...] = jnp.dot(
            left_ref[...],
            right_ref[...],
            preferred_element_type=jnp.float32,
            precision=lax.Precision.HIGHEST,
        )

    pieces = [functools.partial(matrices, step) for step in range(STEPS)]
    pieces += [small, left, right, added]
    rounds = len(far)
    for i, f in enumerate(far):
        if i < len(near):
            pass_on(near[i])
        pass_on(f)
        spread(f).wait_send()
        if i + WINDOW < rounds:
            spread(far[i + WINDOW]).start()
        for piece in pieces[i * len(pieces) // rounds : (i + 1) * len(pieces) // rounds]:
            piece()
    for f in near + far:
        forward(f, other).wait_recv()
    for f in near:
        spread(f).wait_send()
    for f in near + far:
        forward(f, mine).wait_send()


def gather(analysis, zonal, meridional, codes, n):
    comps, levels, own, nx = analysis.shape
    half = ceil_to(own // 2, 16)
    total = ceil_to(comps * (own + half), 32)
    width = nx // n
    rows = levels * (width + 2 * HALO)
    mat_rows = sum(5 * (rows - 4 * levels * (step + 1)) for step in range(STEPS))
    vmem = pl.BlockSpec(memory_space=pltpu.VMEM)
    return pl.pallas_call(
        functools.partial(gather_kernel, n),
        out_shape=(
            jax.ShapeDtypeStruct((n, total, LANES), jnp.bfloat16),
            jax.ShapeDtypeStruct((rows, n * own), jnp.float32),
            jax.ShapeDtypeStruct((mat_rows, rows), jnp.bfloat16),
            jax.ShapeDtypeStruct((rows, 2 * LANES), jnp.bfloat16),
            jax.ShapeDtypeStruct((2, n * own), jnp.float32),
        ),
        in_specs=[pl.BlockSpec(memory_space=pltpu.HBM)] * 4,
        out_specs=(vmem,) * 5,
        scratch_shapes=[pltpu.VMEM((n, total, LANES), jnp.bfloat16)]
        + [pltpu.SemaphoreType.DMA((n,)) for _ in range(4)]
        + [pltpu.VMEM(x.shape, x.dtype) for x in (analysis, zonal, meridional, codes)]
        + [
            pltpu.VMEM((rows, 2 * zonal.size), jnp.float32),
            pltpu.VMEM((2 * zonal.size, n * own), jnp.float32),
            pltpu.SemaphoreType.DMA((4,)),
        ],
        compiler_params=pltpu.CompilerParams(
            collective_id=0, has_side_effects=True, vmem_limit_bytes=24 * 2**20
        ),
    )(analysis, zonal, meridional, codes)


def level_and_column(shape, axis, levels, wide):
    index = lax.broadcasted_iota(jnp.int32, shape, axis)
    level = jnp.zeros(shape, jnp.int32)
    for l in range(1, levels):
        level = level + jnp.where(index >= l * wide, 1, 0)
    return level, index - level * wide


def placing(levels, width):
    wide = width + 2 * HALO
    shape = (levels * wide, 2 * LANES)
    level, x = level_and_column(shape, 0, levels, wide)
    lane = lax.broadcasted_iota(jnp.int32, shape, 1)
    inside = (x >= HALO) & (x < HALO + width)
    main = level * width + x - HALO
    edge = LANES + level * 2 * HALO + jnp.where(x < HALO, x, x - width)
    hit = (lane == jnp.where(inside, main, edge)) | (
        jnp.logical_not(inside) & (lane == edge + LANES // 2)
    )
    return jnp.where(hit, 1.0, 0.0).astype(jnp.bfloat16)


def stencils(levels, wide):
    out = wide - 4
    shape = (levels * out, levels * wide)
    level, x = level_and_column(shape, 0, levels, out)
    from_level, from_x = level_and_column(shape, 1, levels, wide)
    step = from_x - x

    def taps(*values):
        result = jnp.zeros(shape, jnp.float32)
        for i, value in enumerate(values):
            if value:
                result = jnp.where(step == i, float(value), result)
        return result

    same = jnp.where(level == from_level, 1.0, 0.0)
    mix = jnp.where(from_level >= level, 0.5, 0.25)
    slope, mid, smooth = taps(1, -8, 0, 8, -1), taps(0, 0, 1), taps(1, -4, 6, -4, 1)
    blocks = (slope * same, mid * same, smooth * same, slope * mix, mid * mix)
    return [b.astype(jnp.bfloat16) for b in blocks]


def geometry(ny):
    lat = lax.broadcasted_iota(jnp.int32, (1, ny), 1).astype(jnp.float32)
    lat = (math.pi / 3.0) * (2.0 * (lat + 0.5) / ny - 1.0)
    return jnp.concatenate([1.0 / jnp.cos(lat), (2.0 * TIME_STEP) * jnp.sin(lat)], axis=0)


def steps_kernel(dims, r_ref, added_ref, mats_ref, place_ref, geo_ref, out_ref, *refs):
    n, comps, levels, own, half, width = dims
    state_ref, hu_ref, wu_ref, wv_ref, wh_ref, wf_ref = refs
    ny = n * own
    wide = width + 2 * HALO
    rows = levels * wide
    pad = wu_ref.shape[1]

    row_index = lax.broadcasted_iota(jnp.int32, (n, 2 * half, LANES), 1)
    lane_index = lax.broadcasted_iota(jnp.int32, (n, 2 * half, LANES), 2)
    keep = (row_index < half) == (lane_index < LANES // 2)
    for c in range(comps):
        main = r_ref[:, c * own : (c + 1) * own, :]
        start = comps * own + c * half
        edge = r_ref[:, start : start + half, :]
        both = jnp.concatenate([edge, edge], axis=1)
        both = jnp.where(keep, both, jnp.zeros_like(both))
        if 2 * half > own:
            both = jnp.concatenate(
                [both[:, : own - half], both[:, half:]], axis=1
            )
        block = jnp.concatenate([main, both], axis=2).reshape(ny, 2 * LANES)
        field = lax.dot_general(
            place_ref[...], block, (((1,), (1,)), ((), ())), preferred_element_type=jnp.float32
        )
        if c == 0:
            field = field + added_ref[...]
        state_ref[c, :rows, :] = field.astype(jnp.bfloat16)

    for ref in (wu_ref, wv_ref, wh_ref):
        ref[:, ny:] = jnp.zeros((ref.shape[0], pad - ny), jnp.bfloat16)

    base = 0
    for step in range(STEPS):
        rows_in = levels * (wide - 4 * step)
        rows_out = levels * (wide - 4 * step - 4)
        slope_at, mid_at, last_at = base, base + rows_out, base + 5 * rows_out
        wind = mats_ref[slope_at : slope_at + 3 * rows_out, :rows_in]
        thick = mats_ref[mid_at:last_at, :rows_in]
        flux = mats_ref[slope_at:mid_at, :rows_in]
        base = last_at
        column = 1.0 + state_ref[0, :rows_in, :].astype(jnp.float32)
        hu_ref[:rows_in, :] = (column * state_ref[1, :rows_in, :].astype(jnp.float32)).astype(
            jnp.bfloat16
        )

        def times(matrix, x, into):
            into[: matrix.shape[0], :ny] = jnp.dot(
                matrix, x, preferred_element_type=jnp.float32
            ).astype(jnp.bfloat16)

        times(wind, state_ref[1, :rows_in, :], wu_ref)
        times(wind, state_ref[2, :rows_in, :], wv_ref)
        times(thick, state_ref[0, :rows_in, :], wh_ref)
        times(flux, hu_ref[:rows_in, :], wf_ref)

        def group(g, carry, rows_out=rows_out, last=step == STEPS - 1):
            size = 16

            def part(ref, which, lanes=ny):
                first = pl.multiple_of(which * rows_out + g * size, size)
                return ref[pl.ds(first, size), :lanes]

            def around(x):
                return [pltpu.roll(x, s % pad, 1) for s in (2, 1, -1, -2)]

            def slope(near):
                return (8.0 * (near[2] - near[1]) - (near[3] - near[0]))[:, :ny]

            def fourth(x, near):
                return ((near[0] + near[3]) - 4.0 * (near[1] + near[2]) + 6.0 * x)[:, :ny]

            inv = jnp.broadcast_to(geo_ref[0:1, :], (size, ny)).astype(jnp.bfloat16)
            cor = geo_ref[1:2, :]
            h, u, v, p = (
                part(wh_ref, 0, pad),
                part(wu_ref, 1, pad),
                part(wv_ref, 1, pad),
                part(wh_ref, 3, pad),
            )
            ha, ua, va = around(h), around(u), around(v)
            flux_y = slope([a + a * b for a, b in zip(va, ha)])
            press_y = slope(around(p))
            h_s, u_s, v_s = fourth(h, ha), fourth(u, ua), fourth(v, va)
            u_y, v_y = slope(ua), slope(va)
            h, u, v = h[:, :ny], u[:, :ny], v[:, :ny]
            u_x, v_x = part(wu_ref, 0), part(wv_ref, 0)
            ur = u * inv
            k = TIME_STEP / 12.0
            wide_type = jnp.float32
            h_t = inv * part(wf_ref, 0) + flux_y
            u_t = ur * u_x + v * u_y + inv * part(wh_ref, 2)
            v_t = ur * v_x + v * v_y + press_y
            h_s = h_s + part(wh_ref, 1)
            u_s = u_s + part(wu_ref, 2)
            v_s = v_s + part(wv_ref, 2)
            h, u, v, h_t, u_t, v_t, h_s, u_s, v_s = (
                x.astype(wide_type) for x in (h, u, v, h_t, u_t, v_t, h_s, u_s, v_s)
            )
            new_h = h - k * h_t - FILTER * h_s
            new_u = u - k * u_t + cor * v - FILTER * u_s
            new_v = v - k * v_t - cor * u - FILTER * v_s
            here = pl.ds(pl.multiple_of(g * size, size), size)
            target = out_ref if last else state_ref
            for c, value in enumerate((new_h, new_u, new_v)):
                target[c, here, :] = value.astype(jnp.bfloat16)
            return carry

        lax.fori_loop(0, rows_out // 16, group, 0)


def solution(mesh):
    n = mesh.shape["gx"]

    def shards(analysis, zonal, meridional, codes):
        comps, levels, own, nx = analysis.shape
        ny = n * own
        width = nx // n
        wide = width + 2 * HALO
        half = ceil_to(own // 2, 16)
        gathered = gather(analysis, zonal, meridional, codes, n)
        rows_in = levels * wide
        rows_out = rows_in - 4 * levels
        pad = ny + LANES
        vmem = pl.BlockSpec(memory_space=pltpu.VMEM)
        out = pl.pallas_call(
            functools.partial(steps_kernel, (n, comps, levels, own, half, width)),
            out_shape=jax.ShapeDtypeStruct((comps, levels * width, ny), jnp.bfloat16),
            in_specs=[vmem] * 5,
            out_specs=vmem,
            scratch_shapes=[
                pltpu.VMEM((comps, rows_in, ny), jnp.bfloat16),
                pltpu.VMEM((rows_in, ny), jnp.bfloat16),
                pltpu.VMEM((3 * rows_out, pad), jnp.bfloat16),
                pltpu.VMEM((3 * rows_out, pad), jnp.bfloat16),
                pltpu.VMEM((4 * rows_out, pad), jnp.bfloat16),
                pltpu.VMEM((rows_out, ny), jnp.bfloat16),
            ],
            compiler_params=pltpu.CompilerParams(vmem_limit_bytes=48 * 2**20),
        )(*gathered)
        return out.reshape(comps, levels, width, ny)

    placed = (P(None, None, "gx", None), P("member", None), P("member", None), P("member", None))
    return jax.shard_map(
        shards, mesh=mesh, in_specs=placed, out_specs=P("member", None, "gx", None), check_vma=False
    )
```

```python
import functools
import math

import jax
import jax.numpy as jnp
from jax import lax
from jax.experimental import pallas as pl
from jax.experimental.pallas import tpu as pltpu
from jax.sharding import PartitionSpec as P

STEPS = 4
HALO = 2 * STEPS
WINDOW = 3
TIME_STEP = 0.15
FILTER = 0.03
AMP_UNIT = 0.04
LANES = 128
MESH = pl.DeviceIdType.MESH


def ceil_to(value, unit):
    return -(-value // unit) * unit


def turns(product, count):
    rest = product - jnp.floor(product * (1.0 / count)) * count
    return rest * (2.0 * math.pi / count)


def in_row(x, levels):
    x = x.astype(jnp.float32)
    return jnp.concatenate([x[l : l + 1, :] for l in range(levels)], axis=1)


def waves_left(me, nx, width, levels, zonal, codes):
    zonal, codes = in_row(zonal, levels), in_row(codes, levels)
    count = zonal.shape[1]
    zonal = jnp.concatenate([zonal, zonal], axis=1)
    weights = AMP_UNIT * jnp.concatenate([codes, codes], axis=1)
    wide = width + 2 * HALO
    shape = (levels * wide, 2 * count)
    level, x = level_and_column(shape, 0, levels, wide)
    lane = lax.broadcasted_iota(jnp.int32, shape, 1)
    lon = x + (me * width - HALO)
    lon = jnp.where(lon < 0, lon + nx, jnp.where(lon >= nx, lon - nx, lon))
    phase = turns(lon.astype(jnp.float32) * zonal, float(nx))
    modes = count // levels
    sine = lane >= count
    within = lane - jnp.where(sine, count, 0)
    own_level = (within >= level * modes) & (within < level * modes + modes)
    left = jnp.where(sine, -jnp.sin(phase), jnp.cos(phase)) * weights
    return jnp.where(own_level, left, 0.0)


def waves_right(ny, levels, meridional):
    meridional = in_row(meridional, levels)
    count = meridional.shape[1]
    square = (count, count)
    diagonal = lax.broadcasted_iota(jnp.int32, square, 0) == lax.broadcasted_iota(
        jnp.int32, square, 1
    )
    meridional = jnp.sum(
        jnp.where(diagonal, jnp.broadcast_to(meridional, square), 0.0), axis=1, keepdims=True
    )
    lat = lax.broadcasted_iota(jnp.int32, (count, ny), 1).astype(jnp.float32)
    phase = turns(lat * meridional, float(ny))
    return jnp.concatenate([jnp.cos(phase), jnp.sin(phase)], axis=0)


def gather_kernel(
    n,
    x_hbm,
    waves_hbm,
    out_ref,
    mate_ref,
    added_ref,
    mats_ref,
    place_ref,
    geo_ref,
    send_ref,
    send_sem,
    recv_sem,
    fsend_sem,
    frecv_sem,
    msend_sem,
    mrecv_sem,
    x_ref,
    waves_ref,
    left_ref,
    right_ref,
    in_sem,
):
    comps, levels, own, nx = x_ref.shape
    width = nx // n
    total = out_ref.shape[1]
    me = lax.axis_index("gx")
    member = lax.axis_index("member")
    parity = lax.rem(member, 2)
    partner = member + 1 - 2 * parity

    barrier = pltpu.get_barrier_semaphore()
    for off in range(1, n):
        pl.semaphore_signal(
            barrier, inc=1, device_id=(member, lax.rem(me + off, n)), device_id_type=MESH
        )
    pl.semaphore_signal(barrier, inc=1, device_id=(partner, me), device_id_type=MESH)

    size = total // 2
    mine = pl.ds(pl.multiple_of(parity * size, 16), size)
    other = pl.ds(pl.multiple_of((1 - parity) * size, 16), size)
    group = LANES // width
    tiles = nx // LANES
    mine_tile = lax.div(me, group)

    loads = [
        pltpu.make_async_copy(source, target, in_sem.at[i])
        for i, (source, target) in enumerate(
            ((x_hbm, x_ref), (waves_hbm, waves_ref))
        )
    ]
    for load in loads:
        load.start()
    for load in loads:
        load.wait()
    used = (comps + 1) * own
    if total > used:
        send_ref[:, used:, :] = jnp.zeros((n, total - used, LANES), jnp.bfloat16)

    def flipped(value, bits):
        result = value
        b = 1
        while b <= bits:
            if bits & b:
                result = result + b * (1 - 2 * lax.rem(lax.div(value, b), 2))
            b *= 2
        return result

    def tile_columns(c, tile):
        first = pl.multiple_of(tile * LANES, LANES)
        return [x_ref[c, l, :, pl.ds(first, LANES)] for l in range(levels)]

    def pack(tile):
        before = lax.rem(tile + tiles - 1, tiles)
        after = lax.rem(tile + 1, tiles)
        edges = [[] for _ in range(group)]
        for c in range(comps):
            here = tile_columns(c, tile)
            low = [x[:, LANES - HALO :] for x in tile_columns(c, before)]
            high = [x[:, :HALO] for x in tile_columns(c, after)]
            for d in range(group):
                t = tile * group + d
                first = d * width
                last = first + width
                main = [x[:, first:last] for x in here]
                send_ref[t, c * own : (c + 1) * own, :] = jnp.concatenate(main, axis=1)
                for l in range(levels):
                    if d % 2 == 0:
                        edges[d].append(here[l][:, first - HALO : first] if d else low[l])
                    else:
                        edges[d].append(here[l][:, last : last + HALO] if last < LANES else high[l])
        blank = jnp.zeros((own, LANES - comps * levels * HALO), jnp.bfloat16)
        for d in range(group):
            edge = jnp.concatenate(edges[d] + [blank], axis=1)
            send_ref[tile * group + d, comps * own : (comps + 1) * own, :] = edge

    def spread(flip):
        target = flipped(me, flip)
        return pltpu.make_async_remote_copy(
            src_ref=send_ref.at[target, mine],
            dst_ref=out_ref.at[me, mine],
            send_sem=send_sem.at[flip],
            recv_sem=recv_sem.at[flip],
            device_id=(member, target),
            device_id_type=MESH,
        )

    def arrival(flip):
        source = flipped(me, flip)
        return pltpu.make_async_remote_copy(
            src_ref=send_ref.at[source, mine],
            dst_ref=out_ref.at[source, mine],
            send_sem=send_sem.at[flip],
            recv_sem=recv_sem.at[flip],
            device_id=(member, source),
            device_id_type=MESH,
        )

    def forward(flip, rows):
        source = flipped(me, flip)
        return pltpu.make_async_remote_copy(
            src_ref=out_ref.at[source, rows],
            dst_ref=out_ref.at[source, rows],
            send_sem=fsend_sem.at[flip],
            recv_sem=frecv_sem.at[flip],
            device_id=(partner, me),
            device_id_type=MESH,
        )

    mate = flipped(me, 1)

    def share(flip, rows, kind, from_me):
        owner = me if from_me else mate
        source = flipped(owner, flip)
        return pltpu.make_async_remote_copy(
            src_ref=out_ref.at[source, rows],
            dst_ref=mate_ref.at[source, rows],
            send_sem=msend_sem.at[kind, flip],
            recv_sem=mrecv_sem.at[kind, flip],
            device_id=(member, mate),
            device_id_type=MESH,
        )

    whole = pl.ds(0, total)

    order = []
    for tile_flip in range(tiles - 1, -1, -1):
        pack(flipped(mine_tile, tile_flip))
        flips = [tile_flip * group + d for d in range(group - 1, -1, -1)]
        flips = [f for f in flips if f]
        order += flips
        if tile_flip == tiles - 1:
            pl.semaphore_wait(barrier, n)
            for f in flips[:WINDOW]:
                spread(f).start()
        if tile_flip < tiles // 2:
            for f in flips:
                spread(f).start()
    out_ref[me] = send_ref[me]
    share(0, whole, 0, True).start()

    near = [f for f in order if f < n // 2][::-1]
    far = [f for f in order if f >= n // 2]

    def pass_on(flip):
        arrival(flip).wait_recv()
        forward(flip, mine).start()
        share(flip, mine, 0, True).start()

    starts = [0]
    for step in range(STEPS):
        rows = levels * (width + 2 * HALO - 4 * step - 4)
        starts.append(starts[-1] + 5 * rows)

    def matrices(step):
        base = starts[step]
        for block in stencils(levels, width + 2 * HALO - 4 * step):
            mats_ref[base : base + block.shape[0], : block.shape[1]] = block
            base += block.shape[0]

    def small():
        place_ref[...] = placing(comps, levels, width, lax.rem(me, 2))
        geo_ref[...] = geometry(n * own)

    def left():
        left_ref[...] = waves_left(me, nx, width, levels, waves_ref[:levels], waves_ref[2 * levels :])

    def right():
        right_ref[...] = waves_right(n * own, levels, waves_ref[levels : 2 * levels])

    def added():
        added_ref[...] = jnp.dot(
            left_ref[...],
            right_ref[...],
            preferred_element_type=jnp.float32,
            precision=lax.Precision.HIGHEST,
        )

    pieces = [functools.partial(matrices, step) for step in range(STEPS)]
    pieces += [small, left, right, added]
    rounds = len(far)
    for i, f in enumerate(far):
        if i < len(near):
            pass_on(near[i])
        pass_on(f)
        spread(f).wait_send()
        if i + WINDOW < rounds:
            spread(far[i + WINDOW]).start()
        for piece in pieces[i * len(pieces) // rounds : (i + 1) * len(pieces) // rounds]:
            piece()
    for f in near + far:
        forward(f, other).wait_recv()
        share(f, other, 1, True).start()
    for f in near:
        spread(f).wait_send()
    for f in near + far:
        forward(f, mine).wait_send()
    share(0, whole, 0, False).wait_recv()
    share(0, whole, 0, True).wait_send()
    for f in near + far:
        share(f, mine, 0, False).wait_recv()
        share(f, mine, 0, True).wait_send()
        share(f, other, 1, False).wait_recv()
        share(f, other, 1, True).wait_send()


def gather(analysis, zonal, meridional, codes, n):
    comps, levels, own, nx = analysis.shape
    total = ceil_to((comps + 1) * own, 32)
    width = nx // n
    waves = jnp.concatenate([zonal, meridional, codes], axis=0)
    rows = levels * (width + 2 * HALO)
    mat_rows = sum(5 * (rows - 4 * levels * (step + 1)) for step in range(STEPS))
    vmem = pl.BlockSpec(memory_space=pltpu.VMEM)
    return pl.pallas_call(
        functools.partial(gather_kernel, n),
        out_shape=(
            jax.ShapeDtypeStruct((n, total, LANES), jnp.bfloat16),
            jax.ShapeDtypeStruct((n, total, LANES), jnp.bfloat16),
            jax.ShapeDtypeStruct((rows, n * own), jnp.float32),
            jax.ShapeDtypeStruct((mat_rows, rows), jnp.bfloat16),
            jax.ShapeDtypeStruct((comps * rows, 3 * LANES), jnp.bfloat16),
            jax.ShapeDtypeStruct((2, n * own), jnp.float32),
        ),
        in_specs=[pl.BlockSpec(memory_space=pltpu.HBM)] * 2,
        out_specs=(vmem,) * 6,
        scratch_shapes=[pltpu.VMEM((n, total, LANES), jnp.bfloat16)]
        + [pltpu.SemaphoreType.DMA((n,)) for _ in range(4)]
        + [pltpu.SemaphoreType.DMA((2, n)) for _ in range(2)]
        + [pltpu.VMEM(x.shape, x.dtype) for x in (analysis, waves)]
        + [
            pltpu.VMEM((rows, 2 * zonal.size), jnp.float32),
            pltpu.VMEM((2 * zonal.size, n * own), jnp.float32),
            pltpu.SemaphoreType.DMA((2,)),
        ],
        compiler_params=pltpu.CompilerParams(
            collective_id=0, has_side_effects=True, vmem_limit_bytes=24 * 2**20
        ),
    )(analysis, waves)


def level_and_column(shape, axis, levels, wide):
    index = lax.broadcasted_iota(jnp.int32, shape, axis)
    level = jnp.zeros(shape, jnp.int32)
    for l in range(1, levels):
        level = level + jnp.where(index >= l * wide, 1, 0)
    return level, index - level * wide


def placing(comps, levels, width, odd):
    wide = width + 2 * HALO
    shape = (comps * levels * wide, 3 * LANES)
    field, x = level_and_column(shape, 0, comps * levels, wide)
    comp, level = level_and_column(shape, 0, comps, levels * wide)
    level = field - comp * levels
    lane = lax.broadcasted_iota(jnp.int32, shape, 1)
    main = level * width + x - HALO
    edge_low = LANES + field * HALO + x
    edge_high = LANES + field * HALO + x - HALO - width
    mate_low = 2 * LANES + level * width + width - HALO + x
    mate_high = 2 * LANES + level * width + x - HALO - width
    low = jnp.where(odd == 1, mate_low, edge_low)
    high = jnp.where(odd == 1, edge_high, mate_high)
    wanted = jnp.where(x < HALO, low, jnp.where(x < HALO + width, main, high))
    return jnp.where(lane == wanted, 1.0, 0.0).astype(jnp.bfloat16)


def stencils(levels, wide):
    out = wide - 4
    shape = (levels * out, levels * wide)
    level, x = level_and_column(shape, 0, levels, out)
    from_level, from_x = level_and_column(shape, 1, levels, wide)
    step = from_x - x

    def taps(*values):
        result = jnp.zeros(shape, jnp.float32)
        for i, value in enumerate(values):
            if value:
                result = jnp.where(step == i, float(value), result)
        return result

    same = jnp.where(level == from_level, 1.0, 0.0)
    mix = jnp.where(from_level >= level, 0.5, 0.25)
    slope, mid, smooth = taps(1, -8, 0, 8, -1), taps(0, 0, 1), taps(1, -4, 6, -4, 1)
    blocks = (slope * same, mid * same, smooth * same, slope * mix, mid * mix)
    return [b.astype(jnp.bfloat16) for b in blocks]


def geometry(ny):
    lat = lax.broadcasted_iota(jnp.int32, (1, ny), 1).astype(jnp.float32)
    lat = (math.pi / 3.0) * (2.0 * (lat + 0.5) / ny - 1.0)
    return jnp.concatenate([1.0 / jnp.cos(lat), (2.0 * TIME_STEP) * jnp.sin(lat)], axis=0)


def steps_kernel(dims, r_ref, mate_ref, added_ref, mats_ref, place_ref, geo_ref, out_ref, *refs):
    n, comps, levels, own, width = dims
    state_ref, hu_ref, wu_ref, wv_ref, wh_ref, wf_ref = refs
    ny = n * own
    wide = width + 2 * HALO
    rows = levels * wide
    pad = wu_ref.shape[1]

    edge = r_ref[:, comps * own : (comps + 1) * own, :]
    for c in range(comps):
        main = r_ref[:, c * own : (c + 1) * own, :]
        mate = mate_ref[:, c * own : (c + 1) * own, :]
        block = jnp.concatenate([main, edge, mate], axis=2).reshape(ny, 3 * LANES)
        field = lax.dot_general(
            place_ref[c * rows : (c + 1) * rows, :],
            block,
            (((1,), (1,)), ((), ())),
            preferred_element_type=jnp.float32,
        )
        if c == 0:
            field = field + added_ref[...]
        state_ref[c, :rows, :] = field.astype(jnp.bfloat16)

    for ref in (wu_ref, wv_ref, wh_ref):
        ref[:, ny:] = jnp.zeros((ref.shape[0], pad - ny), jnp.bfloat16)

    base = 0
    for step in range(STEPS):
        rows_in = levels * (wide - 4 * step)
        rows_out = levels * (wide - 4 * step - 4)
        slope_at, mid_at, last_at = base, base + rows_out, base + 5 * rows_out
        wind = mats_ref[slope_at : slope_at + 3 * rows_out, :rows_in]
        thick = mats_ref[mid_at:last_at, :rows_in]
        flux = mats_ref[slope_at:mid_at, :rows_in]
        base = last_at
        column = 1.0 + state_ref[0, :rows_in, :].astype(jnp.float32)
        hu_ref[:rows_in, :] = (column * state_ref[1, :rows_in, :].astype(jnp.float32)).astype(
            jnp.bfloat16
        )

        def times(matrix, x, into):
            into[: matrix.shape[0], :ny] = jnp.dot(
                matrix, x, preferred_element_type=jnp.float32
            ).astype(jnp.bfloat16)

        times(wind, state_ref[1, :rows_in, :], wu_ref)
        times(wind, state_ref[2, :rows_in, :], wv_ref)
        times(thick, state_ref[0, :rows_in, :], wh_ref)
        times(flux, hu_ref[:rows_in, :], wf_ref)

        def group(g, carry, rows_out=rows_out, last=step == STEPS - 1):
            size = 16

            def part(ref, which, lanes=ny):
                first = pl.multiple_of(which * rows_out + g * size, size)
                return ref[pl.ds(first, size), :lanes]

            def around(x):
                return [pltpu.roll(x, s % pad, 1) for s in (2, 1, -1, -2)]

            def slope(near):
                return (8.0 * (near[2] - near[1]) - (near[3] - near[0]))[:, :ny]

            def fourth(x, near):
                return ((near[0] + near[3]) - 4.0 * (near[1] + near[2]) + 6.0 * x)[:, :ny]

            inv = jnp.broadcast_to(geo_ref[0:1, :], (size, ny)).astype(jnp.bfloat16)
            cor = geo_ref[1:2, :]
            h, u, v, p = (
                part(wh_ref, 0, pad),
                part(wu_ref, 1, pad),
                part(wv_ref, 1, pad),
                part(wh_ref, 3, pad),
            )
            ha, ua, va = around(h), around(u), around(v)
            flux_y = slope([a + a * b for a, b in zip(va, ha)])
            press_y = slope(around(p))
            h_s, u_s, v_s = fourth(h, ha), fourth(u, ua), fourth(v, va)
            u_y, v_y = slope(ua), slope(va)
            h, u, v = h[:, :ny], u[:, :ny], v[:, :ny]
            u_x, v_x = part(wu_ref, 0), part(wv_ref, 0)
            ur = u * inv
            k = TIME_STEP / 12.0
            wide_type = jnp.float32
            h_t = inv * part(wf_ref, 0) + flux_y
            u_t = ur * u_x + v * u_y + inv * part(wh_ref, 2)
            v_t = ur * v_x + v * v_y + press_y
            h_s = h_s + part(wh_ref, 1)
            u_s = u_s + part(wu_ref, 2)
            v_s = v_s + part(wv_ref, 2)
            h, u, v, h_t, u_t, v_t, h_s, u_s, v_s = (
                x.astype(wide_type) for x in (h, u, v, h_t, u_t, v_t, h_s, u_s, v_s)
            )
            new_h = h - k * h_t - FILTER * h_s
            new_u = u - k * u_t + cor * v - FILTER * u_s
            new_v = v - k * v_t - cor * u - FILTER * v_s
            here = pl.ds(pl.multiple_of(g * size, size), size)
            target = out_ref if last else state_ref
            for c, value in enumerate((new_h, new_u, new_v)):
                target[c, here, :] = value.astype(jnp.bfloat16)
            return carry

        lax.fori_loop(0, rows_out // 16, group, 0)


def solution(mesh):
    n = mesh.shape["gx"]

    def shards(analysis, zonal, meridional, codes):
        comps, levels, own, nx = analysis.shape
        ny = n * own
        width = nx // n
        wide = width + 2 * HALO
        gathered = gather(analysis, zonal, meridional, codes, n)
        rows_in = levels * wide
        rows_out = rows_in - 4 * levels
        pad = ny + LANES
        vmem = pl.BlockSpec(memory_space=pltpu.VMEM)
        out = pl.pallas_call(
            functools.partial(steps_kernel, (n, comps, levels, own, width)),
            out_shape=jax.ShapeDtypeStruct((comps, levels * width, ny), jnp.bfloat16),
            in_specs=[vmem] * 6,
            out_specs=vmem,
            scratch_shapes=[
                pltpu.VMEM((comps, rows_in, ny), jnp.bfloat16),
                pltpu.VMEM((rows_in, ny), jnp.bfloat16),
                pltpu.VMEM((3 * rows_out, pad), jnp.bfloat16),
                pltpu.VMEM((3 * rows_out, pad), jnp.bfloat16),
                pltpu.VMEM((4 * rows_out, pad), jnp.bfloat16),
                pltpu.VMEM((rows_out, ny), jnp.bfloat16),
            ],
            compiler_params=pltpu.CompilerParams(vmem_limit_bytes=48 * 2**20),
        )(*gathered)
        return out.reshape(comps, levels, width, ny)

    placed = (P(None, None, "gx", None), P("member", None), P("member", None), P("member", None))
    return jax.shard_map(
        shards, mesh=mesh, in_specs=placed, out_specs=P("member", None, "gx", None), check_vma=False
    )
```

```python
import functools
import math

import jax
import jax.numpy as jnp
from jax import lax
from jax.experimental import pallas as pl
from jax.experimental.pallas import tpu as pltpu
from jax.sharding import PartitionSpec as P

STEPS = 4
HALO = 2 * STEPS
WINDOW = 3
COLUMNS = 256
TIME_STEP = 0.15
FILTER = 0.03
AMP_UNIT = 0.04
LANES = 128
MESH = pl.DeviceIdType.MESH


def ceil_to(value, unit):
    return -(-value // unit) * unit


def turns(product, count):
    rest = product - jnp.floor(product * (1.0 / count)) * count
    return rest * (2.0 * math.pi / count)


def in_row(x, levels):
    x = x.astype(jnp.float32)
    return jnp.concatenate([x[l : l + 1, :] for l in range(levels)], axis=1)


def waves_left(me, nx, width, levels, zonal, codes):
    zonal, codes = in_row(zonal, levels), in_row(codes, levels)
    count = zonal.shape[1]
    zonal = jnp.concatenate([zonal, zonal], axis=1)
    weights = AMP_UNIT * jnp.concatenate([codes, codes], axis=1)
    wide = width + 2 * HALO
    shape = (levels * wide, 2 * count)
    level, x = level_and_column(shape, 0, levels, wide)
    lane = lax.broadcasted_iota(jnp.int32, shape, 1)
    lon = x + (me * width - HALO)
    lon = jnp.where(lon < 0, lon + nx, jnp.where(lon >= nx, lon - nx, lon))
    phase = turns(lon.astype(jnp.float32) * zonal, float(nx))
    modes = count // levels
    sine = lane >= count
    within = lane - jnp.where(sine, count, 0)
    own_level = (within >= level * modes) & (within < level * modes + modes)
    left = jnp.where(sine, -jnp.sin(phase), jnp.cos(phase)) * weights
    return jnp.where(own_level, left, 0.0)


def waves_right(ny, levels, meridional):
    meridional = in_row(meridional, levels)
    count = meridional.shape[1]
    square = (count, count)
    diagonal = lax.broadcasted_iota(jnp.int32, square, 0) == lax.broadcasted_iota(
        jnp.int32, square, 1
    )
    meridional = jnp.sum(
        jnp.where(diagonal, jnp.broadcast_to(meridional, square), 0.0), axis=1, keepdims=True
    )
    lat = lax.broadcasted_iota(jnp.int32, (count, ny), 1).astype(jnp.float32)
    phase = turns(lat * meridional, float(ny))
    return jnp.concatenate([jnp.cos(phase), jnp.sin(phase)], axis=0)


def gather_kernel(
    n,
    x_ref,
    waves_ref,
    out_ref,
    mate_ref,
    added_ref,
    mats_ref,
    place_ref,
    geo_ref,
    send_ref,
    send_sem,
    recv_sem,
    fsend_sem,
    frecv_sem,
    msend_sem,
    mrecv_sem,
    left_ref,
    right_ref,
):
    comps, levels, own, nx = x_ref.shape
    width = nx // n
    total = out_ref.shape[1]
    me = lax.axis_index("gx")
    member = lax.axis_index("member")
    parity = lax.rem(member, 2)
    partner = member + 1 - 2 * parity

    barrier = pltpu.get_barrier_semaphore()
    for off in range(1, n):
        pl.semaphore_signal(
            barrier, inc=1, device_id=(member, lax.rem(me + off, n)), device_id_type=MESH
        )
    pl.semaphore_signal(barrier, inc=1, device_id=(partner, me), device_id_type=MESH)

    size = total // 2
    mine = pl.ds(pl.multiple_of(parity * size, 16), size)
    other = pl.ds(pl.multiple_of((1 - parity) * size, 16), size)
    group = LANES // width
    tiles = nx // LANES
    mine_tile = lax.div(me, group)

    used = (comps + 1) * own
    if total > used:
        send_ref[:, used:, :] = jnp.zeros((n, total - used, LANES), jnp.bfloat16)

    def flipped(value, bits):
        result = value
        b = 1
        while b <= bits:
            if bits & b:
                result = result + b * (1 - 2 * lax.rem(lax.div(value, b), 2))
            b *= 2
        return result

    def tile_columns(c, tile):
        first = pl.multiple_of(tile * LANES, LANES)
        return [x_ref[c, l, :, pl.ds(first, LANES)] for l in range(levels)]

    def pack(tile):
        before = lax.rem(tile + tiles - 1, tiles)
        after = lax.rem(tile + 1, tiles)
        edges = [[] for _ in range(group)]
        for c in range(comps):
            here = tile_columns(c, tile)
            low = [x[:, LANES - HALO :] for x in tile_columns(c, before)]
            high = [x[:, :HALO] for x in tile_columns(c, after)]
            for d in range(group):
                t = tile * group + d
                first = d * width
                last = first + width
                main = [x[:, first:last] for x in here]
                send_ref[t, c * own : (c + 1) * own, :] = jnp.concatenate(main, axis=1)
                for l in range(levels):
                    if d % 2 == 0:
                        edges[d].append(here[l][:, first - HALO : first] if d else low[l])
                    else:
                        edges[d].append(here[l][:, last : last + HALO] if last < LANES else high[l])
        blank = jnp.zeros((own, LANES - comps * levels * HALO), jnp.bfloat16)
        for d in range(group):
            edge = jnp.concatenate(edges[d] + [blank], axis=1)
            send_ref[tile * group + d, comps * own : (comps + 1) * own, :] = edge

    def spread(flip):
        target = flipped(me, flip)
        return pltpu.make_async_remote_copy(
            src_ref=send_ref.at[target, mine],
            dst_ref=out_ref.at[me, mine],
            send_sem=send_sem.at[flip],
            recv_sem=recv_sem.at[flip],
            device_id=(member, target),
            device_id_type=MESH,
        )

    def arrival(flip):
        source = flipped(me, flip)
        return pltpu.make_async_remote_copy(
            src_ref=send_ref.at[source, mine],
            dst_ref=out_ref.at[source, mine],
            send_sem=send_sem.at[flip],
            recv_sem=recv_sem.at[flip],
            device_id=(member, source),
            device_id_type=MESH,
        )

    def forward(flip, rows):
        source = flipped(me, flip)
        return pltpu.make_async_remote_copy(
            src_ref=out_ref.at[source, rows],
            dst_ref=out_ref.at[source, rows],
            send_sem=fsend_sem.at[flip],
            recv_sem=frecv_sem.at[flip],
            device_id=(partner, me),
            device_id_type=MESH,
        )

    mate = flipped(me, 1)

    def share(flip, rows, kind, from_me):
        owner = me if from_me else mate
        source = flipped(owner, flip)
        return pltpu.make_async_remote_copy(
            src_ref=out_ref.at[source, rows],
            dst_ref=mate_ref.at[source, rows],
            send_sem=msend_sem.at[kind, flip],
            recv_sem=mrecv_sem.at[kind, flip],
            device_id=(member, mate),
            device_id_type=MESH,
        )

    whole = pl.ds(0, total)

    order = []
    for tile_flip in range(tiles - 1, -1, -1):
        pack(flipped(mine_tile, tile_flip))
        flips = [tile_flip * group + d for d in range(group - 1, -1, -1)]
        flips = [f for f in flips if f]
        order += flips
        if tile_flip == tiles - 1:
            pl.semaphore_wait(barrier, n)
            for f in flips[:WINDOW]:
                spread(f).start()
        if tile_flip < tiles // 2:
            for f in flips:
                spread(f).start()
    out_ref[me] = send_ref[me]
    share(0, whole, 0, True).start()

    near = [f for f in order if f < n // 2][::-1]
    far = [f for f in order if f >= n // 2]

    def pass_on(flip):
        arrival(flip).wait_recv()
        forward(flip, mine).start()
        share(flip, mine, 0, True).start()

    starts = [0]
    for step in range(STEPS):
        rows = levels * (width + 2 * HALO - 4 * step - 4)
        starts.append(starts[-1] + 5 * rows)

    def matrices(step):
        base = starts[step]
        for block in stencils(levels, width + 2 * HALO - 4 * step):
            mats_ref[base : base + block.shape[0], : block.shape[1]] = block
            base += block.shape[0]

    def small():
        place_ref[...] = placing(comps, levels, width, lax.rem(me, 2))
        geo_ref[...] = geometry(n * own)

    def left():
        left_ref[...] = waves_left(me, nx, width, levels, waves_ref[:levels], waves_ref[2 * levels :])

    def right():
        right_ref[...] = waves_right(n * own, levels, waves_ref[levels : 2 * levels])

    def added():
        added_ref[...] = jnp.dot(
            left_ref[...],
            right_ref[...],
            preferred_element_type=jnp.float32,
            precision=lax.Precision.HIGHEST,
        )

    pieces = [functools.partial(matrices, step) for step in range(STEPS)]
    pieces += [small, left, right, added]
    rounds = len(far)
    for i, f in enumerate(far):
        if i < len(near):
            pass_on(near[i])
        pass_on(f)
        spread(f).wait_send()
        if i + WINDOW < rounds:
            spread(far[i + WINDOW]).start()
        for piece in pieces[i * len(pieces) // rounds : (i + 1) * len(pieces) // rounds]:
            piece()
    for f in near + far:
        forward(f, other).wait_recv()
        share(f, other, 1, True).start()
    for f in near:
        spread(f).wait_send()
    for f in near + far:
        forward(f, mine).wait_send()
    share(0, whole, 0, False).wait_recv()
    share(0, whole, 0, True).wait_send()
    for f in near + far:
        share(f, mine, 0, False).wait_recv()
        share(f, mine, 0, True).wait_send()
        share(f, other, 1, False).wait_recv()
        share(f, other, 1, True).wait_send()


def gather(analysis, zonal, meridional, codes, n):
    comps, levels, own, nx = analysis.shape
    total = ceil_to((comps + 1) * own, 32)
    width = nx // n
    waves = jnp.concatenate([zonal, meridional, codes], axis=0)
    rows = levels * (width + 2 * HALO)
    mat_rows = sum(5 * (rows - 4 * levels * (step + 1)) for step in range(STEPS))
    vmem = pl.BlockSpec(memory_space=pltpu.VMEM)
    return pl.pallas_call(
        functools.partial(gather_kernel, n),
        out_shape=(
            jax.ShapeDtypeStruct((n, total, LANES), jnp.bfloat16),
            jax.ShapeDtypeStruct((n, total, LANES), jnp.bfloat16),
            jax.ShapeDtypeStruct((rows, n * own), jnp.float32),
            jax.ShapeDtypeStruct((mat_rows, rows), jnp.bfloat16),
            jax.ShapeDtypeStruct((comps * rows, 3 * LANES), jnp.bfloat16),
            jax.ShapeDtypeStruct((2, n * own), jnp.float32),
        ),
        in_specs=[vmem] * 2,
        out_specs=(vmem,) * 6,
        scratch_shapes=[pltpu.VMEM((n, total, LANES), jnp.bfloat16)]
        + [pltpu.SemaphoreType.DMA((n,)) for _ in range(4)]
        + [pltpu.SemaphoreType.DMA((2, n)) for _ in range(2)]
        + [
            pltpu.VMEM((rows, 2 * zonal.size), jnp.float32),
            pltpu.VMEM((2 * zonal.size, n * own), jnp.float32),
        ],
        compiler_params=pltpu.CompilerParams(
            collective_id=0, has_side_effects=True, vmem_limit_bytes=24 * 2**20
        ),
    )(analysis, waves)


def level_and_column(shape, axis, levels, wide):
    index = lax.broadcasted_iota(jnp.int32, shape, axis)
    level = jnp.zeros(shape, jnp.int32)
    for l in range(1, levels):
        level = level + jnp.where(index >= l * wide, 1, 0)
    return level, index - level * wide


def placing(comps, levels, width, odd):
    wide = width + 2 * HALO
    shape = (comps * levels * wide, 3 * LANES)
    field, x = level_and_column(shape, 0, comps * levels, wide)
    comp, level = level_and_column(shape, 0, comps, levels * wide)
    level = field - comp * levels
    lane = lax.broadcasted_iota(jnp.int32, shape, 1)
    main = level * width + x - HALO
    edge_low = LANES + field * HALO + x
    edge_high = LANES + field * HALO + x - HALO - width
    mate_low = 2 * LANES + level * width + width - HALO + x
    mate_high = 2 * LANES + level * width + x - HALO - width
    low = jnp.where(odd == 1, mate_low, edge_low)
    high = jnp.where(odd == 1, edge_high, mate_high)
    wanted = jnp.where(x < HALO, low, jnp.where(x < HALO + width, main, high))
    return jnp.where(lane == wanted, 1.0, 0.0).astype(jnp.bfloat16)


def stencils(levels, wide):
    out = wide - 4
    shape = (levels * out, levels * wide)
    level, x = level_and_column(shape, 0, levels, out)
    from_level, from_x = level_and_column(shape, 1, levels, wide)
    step = from_x - x

    def taps(*values):
        result = jnp.zeros(shape, jnp.float32)
        for i, value in enumerate(values):
            if value:
                result = jnp.where(step == i, float(value), result)
        return result

    same = jnp.where(level == from_level, 1.0, 0.0)
    mix = jnp.where(from_level >= level, 0.5, 0.25)
    slope, mid, smooth = taps(1, -8, 0, 8, -1), taps(0, 0, 1), taps(1, -4, 6, -4, 1)
    blocks = (slope * same, mid * same, smooth * same, slope * mix, mid * mix)
    return [b.astype(jnp.bfloat16) for b in blocks]


def geometry(ny):
    lat = lax.broadcasted_iota(jnp.int32, (1, ny), 1).astype(jnp.float32)
    lat = (math.pi / 3.0) * (2.0 * (lat + 0.5) / ny - 1.0)
    return jnp.concatenate([1.0 / jnp.cos(lat), (2.0 * TIME_STEP) * jnp.sin(lat)], axis=0)


def steps_kernel(dims, r_ref, mate_ref, added_ref, mats_ref, place_ref, geo_ref, out_ref, *refs):
    n, comps, levels, own, width = dims
    state_ref, hu_ref, wu_ref, wv_ref, wh_ref, wf_ref, inv_ref = refs
    ny = n * own
    wide = width + 2 * HALO
    rows = levels * wide
    pad = wu_ref.shape[1]

    edge = r_ref[:, comps * own : (comps + 1) * own, :]
    for c in range(comps):
        main = r_ref[:, c * own : (c + 1) * own, :]
        mate = mate_ref[:, c * own : (c + 1) * own, :]
        block = jnp.concatenate([main, edge, mate], axis=2).reshape(ny, 3 * LANES)
        field = lax.dot_general(
            place_ref[c * rows : (c + 1) * rows, :],
            block,
            (((1,), (1,)), ((), ())),
            preferred_element_type=jnp.float32,
        )
        if c == 0:
            field = field + added_ref[...]
        state_ref[c, :rows, :] = field.astype(jnp.bfloat16)

    for ref in (wu_ref, wv_ref, wh_ref):
        ref[:, ny:] = jnp.zeros((ref.shape[0], pad - ny), jnp.bfloat16)

    inv_ref[...] = jnp.broadcast_to(geo_ref[0:1, :], (16, ny)).astype(jnp.bfloat16)
    base = 0
    for step in range(STEPS):
        rows_in = levels * (wide - 4 * step)
        rows_out = levels * (wide - 4 * step - 4)
        slope_at, mid_at, last_at = base, base + rows_out, base + 5 * rows_out
        wind = mats_ref[slope_at : slope_at + 3 * rows_out, :rows_in]
        thick = mats_ref[mid_at:last_at, :rows_in]
        flux = mats_ref[slope_at:mid_at, :rows_in]
        base = last_at
        column = 1.0 + state_ref[0, :rows_in, :].astype(jnp.float32)
        hu_ref[:rows_in, :] = (column * state_ref[1, :rows_in, :].astype(jnp.float32)).astype(
            jnp.bfloat16
        )

        def times(matrix, x, into):
            for first in range(0, ny, COLUMNS):
                last = min(ny, first + COLUMNS)
                into[: matrix.shape[0], first:last] = jnp.dot(
                    matrix, x[:rows_in, first:last], preferred_element_type=jnp.float32
                ).astype(jnp.bfloat16)

        times(wind, state_ref.at[1], wu_ref)
        times(wind, state_ref.at[2], wv_ref)
        times(thick, state_ref.at[0], wh_ref)
        times(flux, hu_ref, wf_ref)

        def group(g, carry, rows_out=rows_out, last=step == STEPS - 1):
            size = 16

            def part(ref, which, lanes=ny):
                first = pl.multiple_of(which * rows_out + g * size, size)
                return ref[pl.ds(first, size), :lanes]

            def around(x):
                return [pltpu.roll(x, s % pad, 1) for s in (2, 1, -1, -2)]

            def slope(near):
                return (8.0 * (near[2] - near[1]) - (near[3] - near[0]))[:, :ny]

            def fourth(x, near):
                return ((near[0] + near[3]) - 4.0 * (near[1] + near[2]) + 6.0 * x)[:, :ny]

            inv = inv_ref[...]
            cor = geo_ref[1:2, :]
            h, u, v, p = (
                part(wh_ref, 0, pad),
                part(wu_ref, 1, pad),
                part(wv_ref, 1, pad),
                part(wh_ref, 3, pad),
            )
            ha, ua, va = around(h), around(u), around(v)
            flux_y = slope([a + a * b for a, b in zip(va, ha)])
            press_y = slope(around(p))
            h_s, u_s, v_s = fourth(h, ha), fourth(u, ua), fourth(v, va)
            u_y, v_y = slope(ua), slope(va)
            h, u, v = h[:, :ny], u[:, :ny], v[:, :ny]
            u_x, v_x = part(wu_ref, 0), part(wv_ref, 0)
            ur = u * inv
            k = TIME_STEP / 12.0
            wide_type = jnp.float32
            h_t = inv * part(wf_ref, 0) + flux_y
            u_t = ur * u_x + v * u_y + inv * part(wh_ref, 2)
            v_t = ur * v_x + v * v_y + press_y
            h_s = h_s + part(wh_ref, 1)
            u_s = u_s + part(wu_ref, 2)
            v_s = v_s + part(wv_ref, 2)
            h, u, v, h_t, u_t, v_t, h_s, u_s, v_s = (
                x.astype(wide_type) for x in (h, u, v, h_t, u_t, v_t, h_s, u_s, v_s)
            )
            new_h = h - k * h_t - FILTER * h_s
            new_u = u - k * u_t + cor * v - FILTER * u_s
            new_v = v - k * v_t - cor * u - FILTER * v_s
            here = pl.ds(pl.multiple_of(g * size, size), size)
            target = out_ref if last else state_ref
            for c, value in enumerate((new_h, new_u, new_v)):
                target[c, here, :] = value.astype(jnp.bfloat16)
            return carry

        lax.fori_loop(0, rows_out // 16, group, 0)


def solution(mesh):
    n = mesh.shape["gx"]

    def shards(analysis, zonal, meridional, codes):
        comps, levels, own, nx = analysis.shape
        ny = n * own
        width = nx // n
        wide = width + 2 * HALO
        gathered = gather(analysis, zonal, meridional, codes, n)
        rows_in = levels * wide
        rows_out = rows_in - 4 * levels
        pad = ny + LANES
        vmem = pl.BlockSpec(memory_space=pltpu.VMEM)
        out = pl.pallas_call(
            functools.partial(steps_kernel, (n, comps, levels, own, width)),
            out_shape=jax.ShapeDtypeStruct((comps, levels * width, ny), jnp.bfloat16),
            in_specs=[vmem] * 6,
            out_specs=vmem,
            scratch_shapes=[
                pltpu.VMEM((comps, rows_in, ny), jnp.bfloat16),
                pltpu.VMEM((rows_in, ny), jnp.bfloat16),
                pltpu.VMEM((3 * rows_out, pad), jnp.bfloat16),
                pltpu.VMEM((3 * rows_out, pad), jnp.bfloat16),
                pltpu.VMEM((4 * rows_out, pad), jnp.bfloat16),
                pltpu.VMEM((rows_out, ny), jnp.bfloat16),
                pltpu.VMEM((16, ny), jnp.bfloat16),
            ],
            compiler_params=pltpu.CompilerParams(vmem_limit_bytes=32 * 2**20),
        )(*gathered)
        return out.reshape(comps, levels, width, ny)

    placed = (P(None, None, "gx", None), P("member", None), P("member", None), P("member", None))
    return jax.shard_map(
        shards, mesh=mesh, in_specs=placed, out_specs=P("member", None, "gx", None), check_vma=False
    )
```

```python
import functools
import math

import jax
import jax.numpy as jnp
from jax import lax
from jax.experimental import pallas as pl
from jax.experimental.pallas import tpu as pltpu
from jax.sharding import PartitionSpec as P

STEPS = 4
HALO = 2 * STEPS
WINDOW = 4
COLUMNS = 256
TIME_STEP = 0.15
FILTER = 0.03
AMP_UNIT = 0.04
LANES = 128
MESH = pl.DeviceIdType.MESH


def ceil_to(value, unit):
    return -(-value // unit) * unit


def turns(product, count):
    rest = product - jnp.floor(product * (1.0 / count)) * count
    return rest * (2.0 * math.pi / count)


def in_row(x, levels):
    x = x.astype(jnp.float32)
    return jnp.concatenate([x[l : l + 1, :] for l in range(levels)], axis=1)


def waves_left(me, nx, width, levels, zonal, codes):
    zonal, codes = in_row(zonal, levels), in_row(codes, levels)
    count = zonal.shape[1]
    zonal = jnp.concatenate([zonal, zonal], axis=1)
    weights = AMP_UNIT * jnp.concatenate([codes, codes], axis=1)
    wide = width + 2 * HALO
    shape = (levels * wide, 2 * count)
    level, x = level_and_column(shape, 0, levels, wide)
    lane = lax.broadcasted_iota(jnp.int32, shape, 1)
    lon = x + (me * width - HALO)
    lon = jnp.where(lon < 0, lon + nx, jnp.where(lon >= nx, lon - nx, lon))
    phase = turns(lon.astype(jnp.float32) * zonal, float(nx))
    modes = count // levels
    sine = lane >= count
    within = lane - jnp.where(sine, count, 0)
    own_level = (within >= level * modes) & (within < level * modes + modes)
    left = jnp.where(sine, -jnp.sin(phase), jnp.cos(phase)) * weights
    return jnp.where(own_level, left, 0.0)


def waves_right(ny, levels, meridional):
    meridional = in_row(meridional, levels)
    count = meridional.shape[1]
    square = (count, count)
    diagonal = lax.broadcasted_iota(jnp.int32, square, 0) == lax.broadcasted_iota(
        jnp.int32, square, 1
    )
    meridional = jnp.sum(
        jnp.where(diagonal, jnp.broadcast_to(meridional, square), 0.0), axis=1, keepdims=True
    )
    lat = lax.broadcasted_iota(jnp.int32, (count, ny), 1).astype(jnp.float32)
    phase = turns(lat * meridional, float(ny))
    return jnp.concatenate([jnp.cos(phase), jnp.sin(phase)], axis=0)


def gather_kernel(
    n,
    x_ref,
    waves_ref,
    out_ref,
    mate_ref,
    added_ref,
    mats_ref,
    place_ref,
    geo_ref,
    send_ref,
    send_sem,
    recv_sem,
    fsend_sem,
    frecv_sem,
    msend_sem,
    mrecv_sem,
    left_ref,
    right_ref,
):
    comps, levels, own, nx = x_ref.shape
    width = nx // n
    total = out_ref.shape[1]
    me = lax.axis_index("gx")
    member = lax.axis_index("member")
    parity = lax.rem(member, 2)
    partner = member + 1 - 2 * parity

    barrier = pltpu.get_barrier_semaphore()
    for off in range(1, n):
        pl.semaphore_signal(
            barrier, inc=1, device_id=(member, lax.rem(me + off, n)), device_id_type=MESH
        )
    pl.semaphore_signal(barrier, inc=1, device_id=(partner, me), device_id_type=MESH)

    size = total // 2
    mine = pl.ds(pl.multiple_of(parity * size, 16), size)
    other = pl.ds(pl.multiple_of((1 - parity) * size, 16), size)
    group = LANES // width
    tiles = nx // LANES
    mine_tile = lax.div(me, group)

    used = (comps + 1) * own
    if total > used:
        send_ref[:, used:, :] = jnp.zeros((n, total - used, LANES), jnp.bfloat16)

    def flipped(value, bits):
        result = value
        b = 1
        while b <= bits:
            if bits & b:
                result = result + b * (1 - 2 * lax.rem(lax.div(value, b), 2))
            b *= 2
        return result

    def tile_columns(c, tile):
        first = pl.multiple_of(tile * LANES, LANES)
        return [x_ref[c, l, :, pl.ds(first, LANES)] for l in range(levels)]

    def pack(tile):
        before = lax.rem(tile + tiles - 1, tiles)
        after = lax.rem(tile + 1, tiles)
        edges = [[] for _ in range(group)]
        for c in range(comps):
            here = tile_columns(c, tile)
            low = [x[:, LANES - HALO :] for x in tile_columns(c, before)]
            high = [x[:, :HALO] for x in tile_columns(c, after)]
            for d in range(group):
                t = tile * group + d
                first = d * width
                last = first + width
                main = [x[:, first:last] for x in here]
                send_ref[t, c * own : (c + 1) * own, :] = jnp.concatenate(main, axis=1)
                for l in range(levels):
                    if d % 2 == 0:
                        edges[d].append(here[l][:, first - HALO : first] if d else low[l])
                    else:
                        edges[d].append(here[l][:, last : last + HALO] if last < LANES else high[l])
        blank = jnp.zeros((own, LANES - comps * levels * HALO), jnp.bfloat16)
        for d in range(group):
            edge = jnp.concatenate(edges[d] + [blank], axis=1)
            send_ref[tile * group + d, comps * own : (comps + 1) * own, :] = edge

    def spread(flip):
        target = flipped(me, flip)
        return pltpu.make_async_remote_copy(
            src_ref=send_ref.at[target, mine],
            dst_ref=out_ref.at[me, mine],
            send_sem=send_sem.at[flip],
            recv_sem=recv_sem.at[flip],
            device_id=(member, target),
            device_id_type=MESH,
        )

    def arrival(flip):
        source = flipped(me, flip)
        return pltpu.make_async_remote_copy(
            src_ref=send_ref.at[source, mine],
            dst_ref=out_ref.at[source, mine],
            send_sem=send_sem.at[flip],
            recv_sem=recv_sem.at[flip],
            device_id=(member, source),
            device_id_type=MESH,
        )

    def forward(flip, rows):
        source = flipped(me, flip)
        return pltpu.make_async_remote_copy(
            src_ref=out_ref.at[source, rows],
            dst_ref=out_ref.at[source, rows],
            send_sem=fsend_sem.at[flip],
            recv_sem=frecv_sem.at[flip],
            device_id=(partner, me),
            device_id_type=MESH,
        )

    mate = flipped(me, 1)

    def share(flip, rows, kind, from_me):
        owner = me if from_me else mate
        source = flipped(owner, flip)
        return pltpu.make_async_remote_copy(
            src_ref=out_ref.at[source, rows],
            dst_ref=mate_ref.at[source, rows],
            send_sem=msend_sem.at[kind, flip],
            recv_sem=mrecv_sem.at[kind, flip],
            device_id=(member, mate),
            device_id_type=MESH,
        )

    whole = pl.ds(0, total)

    order = []
    for tile_flip in range(tiles - 1, -1, -1):
        pack(flipped(mine_tile, tile_flip))
        flips = [tile_flip * group + d for d in range(group - 1, -1, -1)]
        flips = [f for f in flips if f]
        order += flips
        if tile_flip == tiles - 1:
            pl.semaphore_wait(barrier, n)
            for f in flips[:WINDOW]:
                spread(f).start()
        if tile_flip < tiles // 2:
            for f in flips:
                spread(f).start()
    out_ref[me] = send_ref[me]
    share(0, whole, 0, True).start()

    near = [f for f in order if f < n // 2][::-1]
    far = [f for f in order if f >= n // 2]

    def pass_on(flip):
        arrival(flip).wait_recv()
        forward(flip, mine).start()
        share(flip, mine, 0, True).start()

    starts = [0]
    for step in range(STEPS):
        rows = levels * (width + 2 * HALO - 4 * step - 4)
        starts.append(starts[-1] + 5 * rows)

    def matrices(step):
        base = starts[step]
        for block in stencils(levels, width + 2 * HALO - 4 * step):
            mats_ref[base : base + block.shape[0], : block.shape[1]] = block
            base += block.shape[0]

    def small():
        place_ref[...] = placing(comps, levels, width, lax.rem(me, 2))
        geo_ref[...] = geometry(n * own)

    def left():
        left_ref[...] = waves_left(me, nx, width, levels, waves_ref[:levels], waves_ref[2 * levels :])

    def right():
        right_ref[...] = waves_right(n * own, levels, waves_ref[levels : 2 * levels])

    def added():
        added_ref[...] = jnp.dot(
            left_ref[...],
            right_ref[...],
            preferred_element_type=jnp.float32,
            precision=lax.Precision.HIGHEST,
        )

    pieces = [functools.partial(matrices, step) for step in range(STEPS)]
    pieces += [small, left, right, added]
    rounds = len(far)
    for i, f in enumerate(far):
        if i < len(near):
            pass_on(near[i])
        pass_on(f)
        spread(f).wait_send()
        if i + WINDOW < rounds:
            spread(far[i + WINDOW]).start()
        for piece in pieces[i * len(pieces) // rounds : (i + 1) * len(pieces) // rounds]:
            piece()
    for f in near + far:
        forward(f, other).wait_recv()
        share(f, other, 1, True).start()
    for f in near:
        spread(f).wait_send()
    for f in near + far:
        forward(f, mine).wait_send()
    share(0, whole, 0, False).wait_recv()
    share(0, whole, 0, True).wait_send()
    for f in near + far:
        share(f, mine, 0, False).wait_recv()
        share(f, mine, 0, True).wait_send()
        share(f, other, 1, False).wait_recv()
        share(f, other, 1, True).wait_send()


def gather(analysis, zonal, meridional, codes, n):
    comps, levels, own, nx = analysis.shape
    total = ceil_to((comps + 1) * own, 32)
    width = nx // n
    waves = jnp.concatenate([zonal, meridional, codes], axis=0)
    rows = levels * (width + 2 * HALO)
    mat_rows = sum(5 * (rows - 4 * levels * (step + 1)) for step in range(STEPS))
    vmem = pl.BlockSpec(memory_space=pltpu.VMEM)
    return pl.pallas_call(
        functools.partial(gather_kernel, n),
        out_shape=(
            jax.ShapeDtypeStruct((n, total, LANES), jnp.bfloat16),
            jax.ShapeDtypeStruct((n, total, LANES), jnp.bfloat16),
            jax.ShapeDtypeStruct((rows, n * own), jnp.float32),
            jax.ShapeDtypeStruct((mat_rows, rows), jnp.bfloat16),
            jax.ShapeDtypeStruct((comps * rows, 3 * LANES), jnp.bfloat16),
            jax.ShapeDtypeStruct((2, n * own), jnp.float32),
        ),
        in_specs=[vmem] * 2,
        out_specs=(vmem,) * 6,
        scratch_shapes=[pltpu.VMEM((n, total, LANES), jnp.bfloat16)]
        + [pltpu.SemaphoreType.DMA((n,)) for _ in range(4)]
        + [pltpu.SemaphoreType.DMA((2, n)) for _ in range(2)]
        + [
            pltpu.VMEM((rows, 2 * zonal.size), jnp.float32),
            pltpu.VMEM((2 * zonal.size, n * own), jnp.float32),
        ],
        compiler_params=pltpu.CompilerParams(
            collective_id=0, has_side_effects=True, vmem_limit_bytes=24 * 2**20
        ),
    )(analysis, waves)


def level_and_column(shape, axis, levels, wide):
    index = lax.broadcasted_iota(jnp.int32, shape, axis)
    level = jnp.zeros(shape, jnp.int32)
    for l in range(1, levels):
        level = level + jnp.where(index >= l * wide, 1, 0)
    return level, index - level * wide


def placing(comps, levels, width, odd):
    wide = width + 2 * HALO
    shape = (comps * levels * wide, 3 * LANES)
    field, x = level_and_column(shape, 0, comps * levels, wide)
    comp, level = level_and_column(shape, 0, comps, levels * wide)
    level = field - comp * levels
    lane = lax.broadcasted_iota(jnp.int32, shape, 1)
    main = level * width + x - HALO
    edge_low = LANES + field * HALO + x
    edge_high = LANES + field * HALO + x - HALO - width
    mate_low = 2 * LANES + level * width + width - HALO + x
    mate_high = 2 * LANES + level * width + x - HALO - width
    low = jnp.where(odd == 1, mate_low, edge_low)
    high = jnp.where(odd == 1, edge_high, mate_high)
    wanted = jnp.where(x < HALO, low, jnp.where(x < HALO + width, main, high))
    return jnp.where(lane == wanted, 1.0, 0.0).astype(jnp.bfloat16)


def stencils(levels, wide):
    out = wide - 4
    shape = (levels * out, levels * wide)
    level, x = level_and_column(shape, 0, levels, out)
    from_level, from_x = level_and_column(shape, 1, levels, wide)
    step = from_x - x

    def taps(*values):
        result = jnp.zeros(shape, jnp.float32)
        for i, value in enumerate(values):
            if value:
                result = jnp.where(step == i, float(value), result)
        return result

    same = jnp.where(level == from_level, 1.0, 0.0)
    mix = jnp.where(from_level >= level, 0.5, 0.25)
    slope, mid, smooth = taps(1, -8, 0, 8, -1), taps(0, 0, 1), taps(1, -4, 6, -4, 1)
    blocks = (slope * same, mid * same, smooth * same, slope * mix, mid * mix)
    return [b.astype(jnp.bfloat16) for b in blocks]


def geometry(ny):
    lat = lax.broadcasted_iota(jnp.int32, (1, ny), 1).astype(jnp.float32)
    lat = (math.pi / 3.0) * (2.0 * (lat + 0.5) / ny - 1.0)
    return jnp.concatenate([1.0 / jnp.cos(lat), (2.0 * TIME_STEP) * jnp.sin(lat)], axis=0)


def steps_kernel(dims, r_ref, mate_ref, added_ref, mats_ref, place_ref, geo_ref, out_ref, *refs):
    n, comps, levels, own, width = dims
    state_ref, hu_ref, wu_ref, wv_ref, wh_ref, wf_ref, inv_ref = refs
    ny = n * own
    wide = width + 2 * HALO
    rows = levels * wide
    pad = wu_ref.shape[1]

    edge = r_ref[:, comps * own : (comps + 1) * own, :]
    for c in range(comps):
        main = r_ref[:, c * own : (c + 1) * own, :]
        mate = mate_ref[:, c * own : (c + 1) * own, :]
        block = jnp.concatenate([main, edge, mate], axis=2).reshape(ny, 3 * LANES)
        field = lax.dot_general(
            place_ref[c * rows : (c + 1) * rows, :],
            block,
            (((1,), (1,)), ((), ())),
            preferred_element_type=jnp.float32,
        )
        if c == 0:
            field = field + added_ref[...]
        state_ref[c, :rows, :] = field.astype(jnp.bfloat16)

    for ref in (wu_ref, wv_ref, wh_ref):
        ref[:, ny:] = jnp.zeros((ref.shape[0], pad - ny), jnp.bfloat16)

    inv_ref[...] = jnp.broadcast_to(geo_ref[0:1, :], (16, ny)).astype(jnp.bfloat16)
    base = 0
    for step in range(STEPS):
        rows_in = levels * (wide - 4 * step)
        rows_out = levels * (wide - 4 * step - 4)
        slope_at, mid_at, last_at = base, base + rows_out, base + 5 * rows_out
        wind = mats_ref[slope_at : slope_at + 3 * rows_out, :rows_in]
        thick = mats_ref[mid_at:last_at, :rows_in]
        flux = mats_ref[slope_at:mid_at, :rows_in]
        base = last_at
        column = 1.0 + state_ref[0, :rows_in, :].astype(jnp.float32)
        hu_ref[:rows_in, :] = (column * state_ref[1, :rows_in, :].astype(jnp.float32)).astype(
            jnp.bfloat16
        )

        def times(matrix, x, into):
            for first in range(0, ny, COLUMNS):
                last = min(ny, first + COLUMNS)
                into[: matrix.shape[0], first:last] = jnp.dot(
                    matrix, x[:rows_in, first:last], preferred_element_type=jnp.float32
                ).astype(jnp.bfloat16)

        times(wind, state_ref.at[1], wu_ref)
        times(wind, state_ref.at[2], wv_ref)
        times(thick, state_ref.at[0], wh_ref)
        times(flux, hu_ref, wf_ref)

        def group(g, carry, rows_out=rows_out, last=step == STEPS - 1):
            size = 16

            def part(ref, which, lanes=ny):
                first = pl.multiple_of(which * rows_out + g * size, size)
                return ref[pl.ds(first, size), :lanes]

            def around(x):
                return [pltpu.roll(x, s % pad, 1) for s in (2, 1, -1, -2)]

            def slope(near):
                return (8.0 * (near[2] - near[1]) - (near[3] - near[0]))[:, :ny]

            def fourth(x, near):
                return ((near[0] + near[3]) - 4.0 * (near[1] + near[2]) + 6.0 * x)[:, :ny]

            inv = inv_ref[...]
            cor = geo_ref[1:2, :]
            h, u, v, p = (
                part(wh_ref, 0, pad),
                part(wu_ref, 1, pad),
                part(wv_ref, 1, pad),
                part(wh_ref, 3, pad),
            )
            ha, ua, va = around(h), around(u), around(v)
            flux_y = slope([a + a * b for a, b in zip(va, ha)])
            press_y = slope(around(p))
            h_s, u_s, v_s = fourth(h, ha), fourth(u, ua), fourth(v, va)
            u_y, v_y = slope(ua), slope(va)
            h, u, v = h[:, :ny], u[:, :ny], v[:, :ny]
            u_x, v_x = part(wu_ref, 0), part(wv_ref, 0)
            ur = u * inv
            k = TIME_STEP / 12.0
            wide_type = jnp.float32
            h_t = inv * part(wf_ref, 0) + flux_y
            u_t = ur * u_x + v * u_y + inv * part(wh_ref, 2)
            v_t = ur * v_x + v * v_y + press_y
            h_s = h_s + part(wh_ref, 1)
            u_s = u_s + part(wu_ref, 2)
            v_s = v_s + part(wv_ref, 2)
            h, u, v, h_t, u_t, v_t, h_s, u_s, v_s = (
                x.astype(wide_type) for x in (h, u, v, h_t, u_t, v_t, h_s, u_s, v_s)
            )
            new_h = h - k * h_t - FILTER * h_s
            new_u = u - k * u_t + cor * v - FILTER * u_s
            new_v = v - k * v_t - cor * u - FILTER * v_s
            here = pl.ds(pl.multiple_of(g * size, size), size)
            target = out_ref if last else state_ref
            for c, value in enumerate((new_h, new_u, new_v)):
                target[c, here, :] = value.astype(jnp.bfloat16)
            return carry

        lax.fori_loop(0, rows_out // 16, group, 0)


def solution(mesh):
    n = mesh.shape["gx"]

    def shards(analysis, zonal, meridional, codes):
        comps, levels, own, nx = analysis.shape
        ny = n * own
        width = nx // n
        wide = width + 2 * HALO
        gathered = gather(analysis, zonal, meridional, codes, n)
        rows_in = levels * wide
        rows_out = rows_in - 4 * levels
        pad = ny + LANES
        vmem = pl.BlockSpec(memory_space=pltpu.VMEM)
        out = pl.pallas_call(
            functools.partial(steps_kernel, (n, comps, levels, own, width)),
            out_shape=jax.ShapeDtypeStruct((comps, levels * width, ny), jnp.bfloat16),
            in_specs=[vmem] * 6,
            out_specs=vmem,
            scratch_shapes=[
                pltpu.VMEM((comps, rows_in, ny), jnp.bfloat16),
                pltpu.VMEM((rows_in, ny), jnp.bfloat16),
                pltpu.VMEM((3 * rows_out, pad), jnp.bfloat16),
                pltpu.VMEM((3 * rows_out, pad), jnp.bfloat16),
                pltpu.VMEM((4 * rows_out, pad), jnp.bfloat16),
                pltpu.VMEM((rows_out, ny), jnp.bfloat16),
                pltpu.VMEM((16, ny), jnp.bfloat16),
            ],
            compiler_params=pltpu.CompilerParams(vmem_limit_bytes=32 * 2**20),
        )(*gathered)
        return out.reshape(comps, levels, width, ny)

    placed = (P(None, None, "gx", None), P("member", None), P("member", None), P("member", None))
    return jax.shard_map(
        shards, mesh=mesh, in_specs=placed, out_specs=P("member", None, "gx", None), check_vma=False
    )
```
